32 devices in a mesh: tm: 8 (over y, x, core), mom: 4 (over z).
Axes of the slice: x: 2, y: 2, z: 4, core: 2. Of those that a mesh axis runs over, the one named last changes fastest.
Arguments:
- kernel: bfloat16 [8, 2, 1024, 1024], P('tm'), may hold values from -0.125 to 0.125
- dinv: float32 [8, 2, 1024, 4], P('tm', None, None, 'mom'), may hold values from -0.9 to 0.9
- source: bfloat16 [8, 2, 1024, 4, 256], P('tm', None, None, 'mom'), may hold values from -2.1 to 2.1
- rotation: bfloat16 [4, 8, 8], replicated, may hold values from -1 to 1
- star_of: int32 [4], replicated, may hold values from 0 to 1, as said below
Outputs:
- sigma: bfloat16 [8, 2, 1024, 4, 256], P('tm', None, None, 'mom')
The draws below stay inside these ranges and needn't reach their ends.
Inputs may be any that keep to these rules, and one draw needn't show every extreme that they name: `star_of`: every star 0 .. 1 holds one to three momentum points.
All inputs are finite; a program needn't handle non-finite values.
Results may differ from the reference program's by a relative error of at most 0.024.
Values may be sent and summed in bfloat16 or wider, within the bound.
No kernel may reach another device: no remote copies, remote signals or barrier semaphores. Data moves between devices by JAX's collectives and lax.ppermute only.
A program may use at most 64 MiB of HBM per device.

```python
import jax
import jax.numpy as jnp
from jax import lax

TL = 1024
W = 256
ORB = 8
SECTIONS = 3
KPTS = 4
STARS = 2
STEPS = 128
N_TM = 8


def draw_star_of(key, part):
    label_key, order_key = jax.random.split(jax.random.fold_in(key, 11))
    point_index = jnp.arange(KPTS, dtype=jnp.int32)
    base_star = point_index // 2
    moved_star = jnp.where(point_index % 8 == 2, base_star - 1, base_star).astype(jnp.int32)
    relabel = jax.random.permutation(label_key, jnp.arange(STARS, dtype=jnp.int32))
    labels = jnp.take(relabel, moved_star).astype(jnp.int32)
    return jax.random.permutation(order_key, labels)


def draw_dinv(key, part):
    array_shape = (N_TM, TL, KPTS)
    size_key, phase_key = jax.random.split(jax.random.fold_in(key, 23))
    uniform_draw = jax.random.uniform(size_key, array_shape, jnp.float32)
    magnitude = 0.8 + 0.1 * uniform_draw
    phase_angle = jax.random.uniform(phase_key, array_shape, jnp.float32, -jnp.pi, jnp.pi)
    real_values = magnitude * jnp.cos(phase_angle)
    imag_values = magnitude * jnp.sin(phase_angle)
    return jnp.stack([real_values, imag_values], axis=1).astype(jnp.float32)


def draw_source(key, part):
    array_shape = (N_TM, 2, TL, KPTS, W)
    noise_key = jax.random.fold_in(key, 31)
    tile_index = lax.broadcasted_iota(jnp.int32, array_shape, 0)
    early_tile = tile_index < (N_TM + 4) // 6
    values = jnp.clip(jax.random.normal(noise_key, array_shape, jnp.float32), -6.0, 6.0)
    level_scale = jnp.where(early_tile, 0.35, 0.05)
    return (values * level_scale).astype(jnp.bfloat16)


def draw_rotation(key, part):
    array_shape = (KPTS, ORB, ORB)
    sign_key, diag_key, off_key = jax.random.split(jax.random.fold_in(key, 41), 3)
    row_index = lax.broadcasted_iota(jnp.int32, array_shape, 1)
    column_index = lax.broadcasted_iota(jnp.int32, array_shape, 2)
    on_diagonal = row_index == column_index
    sign_values = jax.random.randint(sign_key, array_shape, 0, 2).astype(jnp.float32) * 2.0 - 1.0
    diag_value = sign_values * jax.random.uniform(diag_key, array_shape, jnp.float32, 0.85, 1.0)
    off_value = jnp.clip(0.1 * jax.random.normal(off_key, array_shape, jnp.float32), -0.4, 0.4)
    return jnp.where(on_diagonal, diag_value, off_value).astype(jnp.bfloat16)


def block_scale(stream_key, dims, cuts, smallest, largest):
    loudness = 1.0
    for position, shards_of in cuts:
        draws = jax.random.uniform(jax.random.fold_in(jax.random.fold_in(stream_key, 6), position), (shards_of,), jnp.float32, smallest / len(cuts), largest / len(cuts))
        loudness = loudness * jnp.repeat(jnp.exp(draws), dims[position] // shards_of).reshape((-1,) + (1,) * (len(dims) - 1 - position))
    return loudness


def gaussian(rng, dims, width, most, cuts=(), kind=jnp.bfloat16):
    values = width * jax.random.normal(rng, dims, jnp.float32)
    if cuts:
        values = values * block_scale(rng, dims, cuts, -0.22, 0.18)
    return jnp.clip(values, -most, most).astype(kind)


def setup_inputs(seed: int = 0) -> dict:
    seeds = jax.random.split(jax.random.key(seed), 6)
    kernel = gaussian(seeds[0], (N_TM, 2, TL, TL), (2 * TL) ** -0.5, 0.125, ((0, 8),))
    dinv = draw_dinv(jax.random.fold_in(seeds[5], 71), 0)
    source = draw_source(jax.random.fold_in(seeds[5], 71), 0)
    rotation = draw_rotation(jax.random.fold_in(seeds[5], 71), 0)
    star_of = draw_star_of(jax.random.fold_in(seeds[5], 71), 0)
    return dict(kernel=kernel, dinv=dinv, source=source, rotation=rotation, star_of=star_of)


def advance(kernel_tile, inverse_diag, basis, incoming):
    shape = incoming.shape
    flat = incoming.reshape(shape[0], shape[1], shape[2] * shape[3])
    real_part = jnp.dot(kernel_tile[0], flat[0], preferred_element_type=jnp.float32) - jnp.dot(kernel_tile[1], flat[1], preferred_element_type=jnp.float32)
    imag_part = jnp.dot(kernel_tile[0], flat[1], preferred_element_type=jnp.float32) + jnp.dot(kernel_tile[1], flat[0], preferred_element_type=jnp.float32)
    total_real = basis[0].astype(jnp.float32) + real_part.reshape(shape[1:])
    total_imag = basis[1].astype(jnp.float32) + imag_part.reshape(shape[1:])
    diag_real = inverse_diag[0][:, :, None]
    diag_imag = inverse_diag[1][:, :, None]
    new_real = diag_real * total_real - diag_imag * total_imag
    new_imag = diag_real * total_imag + diag_imag * total_real
    return jnp.stack([new_real, new_imag]).astype(jnp.bfloat16)


def reference(kernel, dinv, source, rotation, star_of):
    bases = [source[tile_index] for tile_index in range(N_TM)]
    for section_index in range(SECTIONS):
        incoming = jnp.zeros((2, TL, KPTS, W), jnp.bfloat16)
        results = []
        for tile_index in range(N_TM):
            incoming = advance(kernel[tile_index], dinv[tile_index], bases[tile_index], incoming)
            results.append(incoming)
        bases = results
    green = jnp.stack(bases)
    grid = green.astype(jnp.float32).reshape(N_TM, 2, STEPS, ORB, KPTS, W)
    rotation_full = rotation.astype(jnp.float32)
    rotated = jnp.einsum('kab,irtbkw->irtakw', rotation_full, grid, precision=lax.Precision.HIGHEST)
    member = (star_of[None, :] == jnp.arange(STARS, dtype=jnp.int32)[:, None]).astype(jnp.float32)
    mean_weight = member / jnp.sum(member, axis=1, keepdims=True)
    star_green = jnp.einsum('ck,irtakw->irtacw', mean_weight, rotated, precision=lax.Precision.HIGHEST)
    green_real = star_green[:, 0]
    green_imag = star_green[:, 1]
    magnitude = green_real * green_real + green_imag * green_imag
    star_sigma = jnp.stack([magnitude * green_real, magnitude * green_imag], axis=1)
    spread_back = jnp.einsum('ck,irtacw->irtakw', member, star_sigma, precision=lax.Precision.HIGHEST)
    rotated_back = jnp.einsum('kab,irtakw->irtbkw', rotation_full, spread_back, precision=lax.Precision.HIGHEST)
    return rotated_back.reshape(N_TM, 2, TL, KPTS, W).astype(jnp.bfloat16)
```

```python
import functools

import jax
import jax.numpy as jnp
from jax import lax
from jax.experimental import pallas as pl
from jax.experimental.pallas import tpu as pltpu
from jax.sharding import PartitionSpec as P

SECTIONS = 3
LANES = 128
HALF = LANES // 2
DELAY = 2

VMEM = pl.BlockSpec(memory_space=pltpu.VMEM)
ANY = pl.BlockSpec(memory_space=pl.ANY)
F32 = jnp.float32
BF16 = jnp.bfloat16


def params(mib):
    return pltpu.CompilerParams(vmem_limit_bytes=mib * 2**20)


def cost(flops, moved):
    return pl.CostEstimate(flops=flops, bytes_accessed=moved, transcendentals=0)


def lane_index(shape):
    return lax.broadcasted_iota(jnp.int32, shape, len(shape) - 1)


def pack_fronts(source):
    rows, columns = source.shape[1:]
    chunks = columns // LANES

    def body(source_ref, own_ref, send_ref):
        core = lax.rem(lax.axis_index("tm"), 2)
        low = lane_index((rows, LANES)) < HALF
        for target, half in ((own_ref, core), (send_ref, 1 - core)):
            for pair in range(chunks // 2):
                start = pl.multiple_of(half * (columns // 2) + pair * LANES, LANES)
                real = source_ref[0, :, pl.ds(start, LANES)].astype(F32)
                imag = source_ref[1, :, pl.ds(start, LANES)].astype(F32)
                target[2 * pair] = jnp.where(low, real, pltpu.roll(imag, HALF, 1)).astype(BF16)
                target[2 * pair + 1] = jnp.where(low, pltpu.roll(real, HALF, 1), imag).astype(BF16)

    shape = jax.ShapeDtypeStruct((chunks, rows, LANES), BF16)
    return pl.pallas_call(
        body,
        out_shape=(shape, shape),
        in_specs=[VMEM],
        out_specs=(VMEM, VMEM),
        compiler_params=params(16),
        cost_estimate=cost(0, 4 * rows * columns * 2),
        name="pack",
    )(source)


def hold(own, other):
    def body(own_ref, other_ref, out_ref, sems):
        first = pltpu.make_async_copy(own_ref, out_ref.at[0], sems.at[0])
        second = pltpu.make_async_copy(other_ref, out_ref.at[1], sems.at[1])
        first.start()
        second.start()
        first.wait()
        second.wait()

    return pl.pallas_call(
        body,
        out_shape=pltpu.VMEM((2,) + own.shape, own.dtype),
        in_specs=[ANY, ANY],
        out_specs=VMEM,
        scratch_shapes=[pltpu.SemaphoreType.DMA((2,))],
        compiler_params=params(8),
        cost_estimate=cost(0, 4 * own.size * 2),
        name="hold",
    )(own, other)


def tick(time, kernels, factors, own, other, incoming, before):
    rows = incoming.shape[0]
    chunks = own.shape[0]
    items = chunks * SECTIONS
    block = min(rows, 512)

    def body(kernel_ref, factor_ref, own_ref, other_ref, in_ref, prev_a, prev_b, out_a, out_b):
        index = lax.axis_index("tm")
        core = lax.rem(index, 2)
        chip = index // 2
        item = time - DELAY * chip
        chunk = item // SECTIONS
        section = item - chunk * SECTIONS
        sign = jnp.where(lane_index((block, LANES)) < HALF, -1.0, 1.0).astype(F32)

        def finish(slot, start, total, target):
            span = pl.ds(start, block)
            turned = pltpu.roll(total, HALF, 1) * sign
            target[span, :] = (factor_ref[slot, 0, span, :] * total + factor_ref[slot, 1, span, :] * turned).astype(BF16)

        def product(slot, start, x_ref):
            real = jnp.dot(kernel_ref[slot, pl.ds(start, block), :], x_ref[...], preferred_element_type=F32)
            imag = jnp.dot(kernel_ref[slot, pl.ds(rows + start, block), :], x_ref[...], preferred_element_type=F32)
            return real + pltpu.roll(imag, HALF, 1) * sign

        @pl.when((item >= 0) & (item < items))
        def _():
            @pl.when(section == 0)
            def _():
                @pl.when(core == 0)
                def _():
                    prev_a[...] = own_ref[chunk]
                    prev_b[...] = other_ref[chunk]

                @pl.when(core == 1)
                def _():
                    prev_a[...] = other_ref[chunk]
                    prev_b[...] = own_ref[chunk]

            @pl.when(chip == 0)
            def _():
                for start in range(0, rows, block):
                    finish(core, start, prev_a[pl.ds(start, block), :].astype(F32), out_a)

            @pl.when(chip > 0)
            def _():
                for start in range(0, rows, block):
                    total = prev_a[pl.ds(start, block), :].astype(F32) + product(core, start, in_ref)
                    finish(core, start, total, out_a)

            for start in range(0, rows, block):
                total = prev_b[pl.ds(start, block), :].astype(F32) + product(1 - core, start, out_a)
                finish(1 - core, start, total, out_b)

    def body_with_scratch(kernel_ref, factor_ref, own_ref, other_ref, in_ref, before_a, before_b, out_a, out_b, prev_a, prev_b):
        section = lax.rem(time - DELAY * (lax.axis_index("tm") // 2) + SECTIONS * 64, SECTIONS)

        @pl.when(section > 0)
        def _():
            prev_a[...] = before_a[...]
            prev_b[...] = before_b[...]

        body(kernel_ref, factor_ref, own_ref, other_ref, in_ref, prev_a, prev_b, out_a, out_b)

    shape = jax.ShapeDtypeStruct((rows, LANES), BF16)
    return pl.pallas_call(
        body_with_scratch,
        out_shape=(shape, shape),
        in_specs=[VMEM] * 7,
        out_specs=(VMEM, VMEM),
        scratch_shapes=[pltpu.VMEM((rows, LANES), BF16)] * 2,
        compiler_params=params(8),
        cost_estimate=cost(2 * 4 * rows * rows * 256, 8 * rows * LANES),
        name="tick",
    )(kernels, factors, own, other, incoming, *before)


def collect(candidates, chunks, stages):
    rows = candidates[0].shape[0]

    def body(*refs):
        inputs = refs[: len(candidates)]
        keep_ref, send_ref, sems = refs[len(candidates) :]
        index = lax.axis_index("tm")
        core = lax.rem(index, 2)
        chip = index // 2
        for stage in range(stages):
            for parity in range(2):

                @pl.when((chip == stage) & (core == parity))
                def _():
                    copies = []
                    for chunk in range(chunks):
                        base = (stage * chunks + chunk) * 2
                        copies.append(pltpu.make_async_copy(inputs[base + parity], keep_ref.at[chunk], sems.at[2 * chunk]))
                        copies.append(pltpu.make_async_copy(inputs[base + 1 - parity], send_ref.at[chunk], sems.at[2 * chunk + 1]))
                    for copy in copies:
                        copy.start()
                    for copy in copies:
                        copy.wait()

    shape = jax.ShapeDtypeStruct((chunks, rows, LANES), BF16)
    return pl.pallas_call(
        body,
        out_shape=(shape, shape),
        in_specs=[ANY] * len(candidates),
        out_specs=(VMEM, VMEM),
        scratch_shapes=[pltpu.SemaphoreType.DMA((2 * chunks,))],
        compiler_params=params(8),
        cost_estimate=cost(0, 4 * chunks * rows * LANES * 2),
        name="collect",
    )(*candidates)


def star_stage(panels, forward, backward, weights, stars):
    points, pieces, rows, _ = panels.shape
    span = forward.shape[0] // stars

    def body(panel_ref, forward_ref, backward_ref, weight_ref, out_ref):
        for piece in range(pieces):
            for start in range(0, rows, span):
                block = panel_ref[:, piece, pl.ds(start, span), :].reshape(points * span, LANES)
                green = jnp.dot(forward_ref[...], block, preferred_element_type=F32) * weight_ref[...]
                square = green * green
                sigma = (square + pltpu.roll(square, HALF, 1)) * green
                high = sigma.astype(BF16)
                low = (sigma - high.astype(F32)).astype(BF16)
                back = jnp.dot(backward_ref[...], high, preferred_element_type=F32)
                back += jnp.dot(backward_ref[...], low, preferred_element_type=F32)
                out_ref[:, piece, pl.ds(start, span), :] = back.astype(BF16).reshape(points, span, LANES)

    return pl.pallas_call(
        body,
        out_shape=jax.ShapeDtypeStruct(panels.shape, BF16),
        in_specs=[VMEM] * 4,
        out_specs=VMEM,
        compiler_params=params(16),
        cost_estimate=cost(2 * panels.size * 3 * stars * span, 4 * panels.size),
        name="stars",
    )(panels, forward, backward, weights)


def unpack(panels, columns):
    owners, pieces, panel_rows, _ = panels.shape

    def body(panel_ref, out_ref):
        core = lax.rem(lax.axis_index("tm"), 2)
        low = lane_index((panel_rows, LANES)) < HALF
        for side, half in ((0, core), (1, 1 - core)):
            for pair in range(pieces // 4):
                start = pl.multiple_of(half * (columns // 2) + pair * LANES, LANES)
                for owner in range(owners):
                    first = panel_ref[owner, side * (pieces // 2) + 2 * pair].astype(F32)
                    second = panel_ref[owner, side * (pieces // 2) + 2 * pair + 1].astype(F32)
                    span = pl.ds(owner * panel_rows, panel_rows)
                    out_ref[0, span, pl.ds(start, LANES)] = jnp.where(low, first, pltpu.roll(second, HALF, 1)).astype(BF16)
                    out_ref[1, span, pl.ds(start, LANES)] = jnp.where(low, pltpu.roll(first, HALF, 1), second).astype(BF16)

    return pl.pallas_call(
        body,
        out_shape=jax.ShapeDtypeStruct((2, owners * panel_rows, columns), BF16),
        in_specs=[VMEM],
        out_specs=VMEM,
        compiler_params=params(16),
        cost_estimate=cost(0, 4 * panels.size),
        name="unpack",
    )(panels)


def star_tables(rotation, star_of, span):
    points, orbitals = rotation.shape[:2]
    stars = points // 2
    member = star_of[None, :] == jnp.arange(stars, dtype=jnp.int32)[:, None]
    same = jnp.eye(span // orbitals, dtype=bool)
    keep = member[:, None, None, :, None, None] & same[None, :, None, None, :, None]
    spread = jnp.where(keep, jnp.transpose(rotation, (1, 0, 2))[None, None, :, :, None, :], 0)
    forward = spread.reshape(stars * span, points * span).astype(BF16)
    weight = 1.0 / jnp.sum(member.astype(F32), axis=1)
    weights = jnp.broadcast_to(weight[:, None, None], (stars, span, LANES)).reshape(stars * span, LANES)
    return forward, forward.T, weights, stars


def shards(kernel, dinv, source, rotation, star_of):
    tiles = lax.axis_size("tm")
    owners = lax.axis_size("mom")
    rows = source.shape[2]
    columns = source.shape[4]
    stages = tiles // 2
    chunks = columns // LANES
    items = chunks * SECTIONS
    trade = functools.partial(lax.ppermute, axis_name="tm", perm=[(i, i ^ 1) for i in range(tiles)])
    onward = functools.partial(lax.ppermute, axis_name="tm", perm=[(i, i + 2) for i in range(tiles - 2)])

    own_kernel = kernel.reshape(2 * rows, rows)
    other_kernel = trade(own_kernel)
    own, send = pack_fronts(source.reshape(2, rows, columns))
    other = trade(send)
    own_dinv = dinv.reshape(2, rows)
    both = jnp.stack([own_dinv, trade(own_dinv)])
    factors = jnp.broadcast_to(both[..., None], (2, 2, rows, LANES))
    kernels = hold(own_kernel, other_kernel)

    incoming = [own[0]] * DELAY
    before = (own[0], own[0])
    solved = []
    for time in range(items + DELAY * (stages - 1)):
        before = tick(time, kernels, factors, own, other, incoming[time], before)
        solved.append(before)
        incoming.append(onward(before[1]))

    candidates = []
    for stage in range(stages):
        for chunk in range(chunks):
            candidates.extend(solved[DELAY * stage + SECTIONS * chunk + SECTIONS - 1])
    keep, give = collect(candidates, chunks, stages)
    got = trade(give)
    green = jnp.concatenate([keep, got])

    forward, backward, weights, stars = star_tables(rotation, star_of, LANES)
    pieces = 2 * chunks
    panels = green.reshape(pieces, owners, rows // owners, LANES).transpose(1, 0, 2, 3)
    panels = lax.all_to_all(panels, "mom", 0, 0, tiled=True)
    panels = star_stage(panels, forward, backward, weights, stars)
    panels = lax.all_to_all(panels, "mom", 0, 0, tiled=True)
    return unpack(panels, columns).reshape(1, 2, rows, 1, columns)


def solution(mesh):
    in_specs = (
        P("tm", None, None, None),
        P("tm", None, None, "mom"),
        P("tm", None, None, "mom", None),
        P(),
        P(),
    )
    out_specs = P("tm", None, None, "mom", None)
    return jax.shard_map(shards, mesh=mesh, in_specs=in_specs, out_specs=out_specs, check_vma=False)
```

```python
import functools

import jax
import jax.numpy as jnp
from jax import lax
from jax.experimental import pallas as pl
from jax.experimental.pallas import tpu as pltpu
from jax.sharding import PartitionSpec as P

SECTIONS = 3
LANES = 128
HALF = LANES // 2
DELAY = 2

VMEM = pl.BlockSpec(memory_space=pltpu.VMEM)
ANY = pl.BlockSpec(memory_space=pl.ANY)
F32 = jnp.float32
BF16 = jnp.bfloat16


def params(mib):
    return pltpu.CompilerParams(vmem_limit_bytes=mib * 2**20)


def cost(flops, moved):
    return pl.CostEstimate(flops=flops, bytes_accessed=moved, transcendentals=0)


def lane_index(shape):
    return lax.broadcasted_iota(jnp.int32, shape, len(shape) - 1)


def turn(x, shift, half=HALF):
    shift %= half
    if shift == 0:
        return x
    inside = lax.rem(lane_index(x.shape), half) >= shift
    return jnp.where(inside, pltpu.roll(x, shift, 1), pltpu.roll(x, shift + half, 1))


def lane_block(shape, owners):
    return lax.rem(lane_index(shape), HALF) // (HALF // owners)


def wrap(x, owners):
    return lax.rem(x + 2 * owners, owners)


def to_messages(blocks, owners, place, store):
    width = HALF // owners
    turned = [turn(block, width * q) for q, block in enumerate(blocks)]
    lanes = lane_block(blocks[0].shape, owners)
    for step in range(owners):
        panel = wrap(lanes - place - step, owners)
        message = turned[0]
        for q in range(1, owners):
            message = jnp.where(panel == q, turned[q], message)
        store(step, message.astype(BF16))


def from_messages(messages, owners, place):
    width = HALF // owners
    turned = [turn(message.astype(F32), width * ((owners - step) % owners)) for step, message in enumerate(messages)]
    lanes = lane_block(messages[0].shape, owners)
    panels = []
    for q in range(owners):
        step_of = wrap(place - lanes + q, owners)
        panel = turned[0]
        for step in range(1, owners):
            panel = jnp.where(step_of == step, turned[step], panel)
        panels.append(turn(panel, HALF - width * q))
    return panels


def pack_fronts(source, dinv, owners):
    rows, columns = source.shape[1:]
    chunks = columns // LANES
    panel = rows // owners
    extra = 3 * dinv.shape[0]

    def body(source_ref, dinv_ref, *out_refs):
        core = lax.rem(lax.axis_index("tm"), 2)
        place = lax.axis_index("mom")
        low = lane_index((panel, LANES)) < HALF
        first = dinv_ref[...].astype(BF16)
        rest = dinv_ref[...] - first.astype(F32)
        second = rest.astype(BF16)
        third = (rest - second.astype(F32)).astype(BF16)
        pieces = jnp.concatenate([first, second, third])
        for slot in range(2):
            half = core if slot == 0 else 1 - core
            for step in range(owners):
                out_refs[step][slot, pl.ds(panel, extra), :] = pieces
            for pair in range(chunks // 2):
                start = pl.multiple_of(half * (columns // 2) + pair * LANES, LANES)
                even, odd = [], []
                for q in range(owners):
                    real = source_ref[0, pl.ds(q * panel, panel), pl.ds(start, LANES)].astype(F32)
                    imag = source_ref[1, pl.ds(q * panel, panel), pl.ds(start, LANES)].astype(F32)
                    even.append(jnp.where(low, real, pltpu.roll(imag, HALF, 1)))
                    odd.append(jnp.where(low, pltpu.roll(real, HALF, 1), imag))
                for chunk, blocks in ((2 * pair, even), (2 * pair + 1, odd)):

                    def store(step, message):
                        out_refs[chunk * owners + step][slot, pl.ds(0, panel), :] = message

                    to_messages(blocks, owners, place, store)

    shapes = []
    for chunk in range(chunks):
        height = panel + (extra if chunk == 0 else 0)
        shapes.extend([jax.ShapeDtypeStruct((2, height, LANES), BF16)] * owners)
    return pl.pallas_call(
        body,
        out_shape=tuple(shapes),
        in_specs=[VMEM, VMEM],
        out_specs=(VMEM,) * len(shapes),
        compiler_params=params(16),
        cost_estimate=cost(0, 4 * rows * columns * 2),
        name="pack",
    )(source, dinv)


def unpack_fronts(kept, got, rows, with_factors):
    owners = len(kept)
    panel = rows // owners
    blocks = rows // LANES
    extra = kept[0].shape[1] - panel

    def body(*refs):
        kept_refs, got_refs, outs = refs[:owners], refs[owners : 2 * owners], refs[2 * owners :]
        place = lax.axis_index("mom")
        for tile in range(2):
            read = (lambda step, span: kept_refs[step][0, span, :]) if tile == 0 else (lambda step, span: got_refs[step][span, :])
            panels = from_messages([read(step, pl.ds(0, panel)) for step in range(owners)], owners, place)
            for q in range(owners):
                outs[tile][pl.ds(q * panel, panel), :] = panels[q].astype(BF16)
            if not with_factors:
                continue
            pieces = jnp.concatenate([read(step, pl.ds(panel, extra)) for step in range(owners)])
            shape = (owners * extra, LANES)
            row = lax.broadcasted_iota(jnp.int32, shape, 0)
            owner = wrap(place - row // extra, owners)
            wanted = owner == lane_block(shape, owners)
            inner = lax.rem(lax.rem(row, extra), 2 * blocks)
            sign = jnp.where(lane_index(shape) < HALF, -1.0, 1.0)
            for part in range(2):
                scale = jnp.ones(shape, F32) if part == 0 else sign
                for block in range(blocks):
                    pick = jnp.where(wanted & (inner == part * blocks + block), scale, 0.0).astype(BF16)
                    spread = lax.dot_general(pieces, pick, (((0,), (0,)), ((), ())), preferred_element_type=F32)
                    outs[2][tile, part, pl.ds(block * LANES, LANES), :] = spread

    shapes = [jax.ShapeDtypeStruct((rows, LANES), BF16)] * 2
    if with_factors:
        shapes.append(pltpu.VMEM((2, 2, rows, LANES), F32))
    return pl.pallas_call(
        body,
        out_shape=tuple(shapes),
        in_specs=[VMEM] * (2 * owners),
        out_specs=(VMEM,) * len(shapes),
        compiler_params=params(16),
        cost_estimate=cost(0, 8 * rows * LANES),
        name="unpack_first" if with_factors else "unpack_next",
    )(*kept, *got)


def hold(own, other):
    def body(own_ref, other_ref, out_ref, sems):
        first = pltpu.make_async_copy(own_ref, out_ref.at[0], sems.at[0])
        second = pltpu.make_async_copy(other_ref, out_ref.at[1], sems.at[1])
        first.start()
        second.start()
        first.wait()
        second.wait()

    return pl.pallas_call(
        body,
        out_shape=pltpu.VMEM((2,) + own.shape, own.dtype),
        in_specs=[ANY, ANY],
        out_specs=VMEM,
        scratch_shapes=[pltpu.SemaphoreType.DMA((2,))],
        compiler_params=params(8),
        cost_estimate=cost(0, 4 * own.size * 2),
        name="hold",
    )(own, other)


def tick(time, kernels, factors, fronts, incoming, before, items):
    rows = incoming.shape[0]
    block = min(rows, 512)
    chunks = sorted(fronts)

    def body(kernel_ref, factor_ref, in_ref, *refs):
        front_refs = refs[: 2 * len(chunks)]
        before_a, before_b, out_a, out_b, base_a, base_b = refs[2 * len(chunks) :]
        index = lax.axis_index("tm")
        core = lax.rem(index, 2)
        chip = index // 2
        item = time - DELAY * chip
        section = lax.rem(item + SECTIONS * 64, SECTIONS)
        sign = jnp.where(lane_index((block, LANES)) < HALF, -1.0, 1.0).astype(F32)

        def finish(slot, start, total, target):
            span = pl.ds(start, block)
            turned = pltpu.roll(total, HALF, 1)
            target[span, :] = (factor_ref[slot, 0, span, :] * total + factor_ref[slot, 1, span, :] * turned).astype(BF16)

        def product(slot, start, x_ref):
            real = jnp.dot(kernel_ref[slot, pl.ds(start, block), :], x_ref[...], preferred_element_type=F32)
            imag = jnp.dot(kernel_ref[slot, pl.ds(rows + start, block), :], x_ref[...], preferred_element_type=F32)
            return real + pltpu.roll(imag, HALF, 1) * sign

        @pl.when((item >= 0) & (item < items))
        def _():
            for place, chunk in enumerate(chunks):
                for parity in range(2):

                    @pl.when((item == chunk * SECTIONS) & (core == parity))
                    def _():
                        base_a[...] = front_refs[2 * place + parity][...]
                        base_b[...] = front_refs[2 * place + 1 - parity][...]

            @pl.when(section > 0)
            def _():
                base_a[...] = before_a[...]
                base_b[...] = before_b[...]

            @pl.when(chip == 0)
            def _():
                for start in range(0, rows, block):
                    finish(core, start, base_a[pl.ds(start, block), :].astype(F32), out_a)

            @pl.when(chip > 0)
            def _():
                for start in range(0, rows, block):
                    total = base_a[pl.ds(start, block), :].astype(F32) + product(core, start, in_ref)
                    finish(core, start, total, out_a)

            for start in range(0, rows, block):
                total = base_b[pl.ds(start, block), :].astype(F32) + product(1 - core, start, out_a)
                finish(1 - core, start, total, out_b)

    shape = jax.ShapeDtypeStruct((rows, LANES), BF16)
    given = [front for chunk in chunks for front in fronts[chunk]]
    return pl.pallas_call(
        body,
        out_shape=(shape, shape),
        in_specs=[VMEM] * (5 + len(given)),
        out_specs=(VMEM, VMEM),
        scratch_shapes=[pltpu.VMEM((rows, LANES), BF16)] * 2,
        compiler_params=params(8),
        cost_estimate=cost(2 * 4 * rows * rows * 256, 8 * rows * LANES),
        name="tick",
    )(kernels, factors, incoming, *given, *before)


def star_stage(candidates, forward, backward, weights, owners):
    rows = candidates[0].shape[0]
    stages = len(candidates) // 2
    panel = rows // owners
    orbitals = forward.shape[0]
    width = HALF // owners

    def body(*refs):
        inputs = refs[: len(candidates)]
        forward_ref, backward_ref, weight_ref = refs[len(candidates) : len(candidates) + 3]
        out_refs = refs[len(candidates) + 3 : len(candidates) + 3 + owners]
        green_ref, sems = refs[len(candidates) + 3 + owners :]
        index = lax.axis_index("tm")
        core = lax.rem(index, 2)
        chip = index // 2
        place = lax.axis_index("mom")
        for stage in range(stages):
            for parity in range(2):

                @pl.when((chip == stage) & (core == parity))
                def _():
                    copies = [
                        pltpu.make_async_copy(inputs[2 * stage + (parity + slot) % 2], green_ref.at[slot], sems.at[slot])
                        for slot in range(2)
                    ]
                    for copy in copies:
                        copy.start()
                    for copy in copies:
                        copy.wait()

        def mix(x, table_ref):
            groups = x.reshape(panel // orbitals, orbitals, LANES)
            total = groups * table_ref[0]
            for shift in range(1, orbitals):
                total += pltpu.roll(groups, shift, 1) * table_ref[shift]
            return total.reshape(panel, LANES)

        for slot in range(2):
            blocks = []
            for q in range(owners):
                rotated = mix(green_ref[slot, pl.ds(q * panel, panel), :].astype(F32), forward_ref)
                green = rotated * weight_ref[0]
                for step in range(1, owners):
                    green += turn(rotated, width * step) * weight_ref[step]
                square = green * green
                sigma = (square + pltpu.roll(square, HALF, 1)) * green
                blocks.append(mix(sigma, backward_ref))

            def store(step, message):
                out_refs[step][slot] = message

            to_messages(blocks, owners, place, store)

    shape = jax.ShapeDtypeStruct((2, panel, LANES), BF16)
    return pl.pallas_call(
        body,
        out_shape=(shape,) * owners,
        in_specs=[ANY] * len(candidates) + [VMEM] * 3,
        out_specs=(VMEM,) * owners,
        scratch_shapes=[pltpu.VMEM((2, rows, LANES), BF16), pltpu.SemaphoreType.DMA((2,))],
        compiler_params=params(16),
        cost_estimate=cost(0, 16 * rows * LANES),
        name="stars",
    )(*candidates, forward, backward, weights)


def assemble(chunked, columns):
    owners = len(chunked[0][0])
    panel = chunked[0][0][0].shape[1]

    def body(*refs):
        out_ref = refs[-1]
        core = lax.rem(lax.axis_index("tm"), 2)
        place = lax.axis_index("mom")
        low = lane_index((panel, LANES)) < HALF
        for side in range(2):
            half = core if side == 0 else 1 - core
            for pair in range(len(chunked) // 2):
                start = pl.multiple_of(half * (columns // 2) + pair * LANES, LANES)
                both = []
                for chunk in (2 * pair, 2 * pair + 1):
                    base = (2 * chunk + side) * owners
                    messages = [refs[base + d][0] if side == 0 else refs[base + d][...] for d in range(owners)]
                    both.append(from_messages(messages, owners, place))
                for q in range(owners):
                    first, second = both[0][q], both[1][q]
                    span = pl.ds(q * panel, panel)
                    out_ref[0, span, pl.ds(start, LANES)] = jnp.where(low, first, pltpu.roll(second, HALF, 1)).astype(BF16)
                    out_ref[1, span, pl.ds(start, LANES)] = jnp.where(low, pltpu.roll(first, HALF, 1), second).astype(BF16)

    given = [message for kept, got in chunked for message in (*kept, *got)]
    return pl.pallas_call(
        body,
        out_shape=jax.ShapeDtypeStruct((2, owners * panel, columns), BF16),
        in_specs=[VMEM] * len(given),
        out_specs=VMEM,
        compiler_params=params(16),
        cost_estimate=cost(0, 8 * owners * panel * columns),
        name="assemble",
    )(*given)


def star_tables(rotation, star_of):
    points, orbitals = rotation.shape[:2]
    width = HALF // points

    def spread(x):
        shape = x.shape[:-1] + (2, points, width)
        return jnp.broadcast_to(x[..., None, :, None], shape).reshape(x.shape[:-1] + (LANES,))

    lanes = spread(jnp.transpose(rotation.astype(F32), (1, 2, 0)))
    index = jnp.arange(orbitals)
    pick = (index[None, None, :] == (index[None, :, None] - index[:, None, None]) % orbitals).astype(F32)
    forward = jnp.sum(pick[..., None] * lanes[None], axis=2)
    backward = jnp.sum(pick[..., None] * jnp.swapaxes(lanes, 0, 1)[None], axis=2)
    same = (star_of[:, None] == star_of[None, :]).astype(F32)
    mean = same / jnp.sum(same, axis=1, keepdims=True)
    point = jnp.arange(points)
    distance = (point[None, None, :] == (point[None, :, None] - point[:, None, None]) % points).astype(F32)
    weights = spread(jnp.sum(mean[None] * distance, axis=2))
    return forward, backward, weights[:, None, :]


def shards(kernel, dinv, source, rotation, star_of):
    tiles = lax.axis_size("tm")
    owners = lax.axis_size("mom")
    rows = source.shape[2]
    columns = source.shape[4]
    stages = tiles // 2
    chunks = columns // LANES
    items = chunks * SECTIONS
    trade = functools.partial(lax.ppermute, axis_name="tm", perm=[(i, i ^ 1) for i in range(tiles)])
    onward = functools.partial(lax.ppermute, axis_name="tm", perm=[(i, i + 2) for i in range(tiles - 2)])

    def exchange(messages):
        kept = [messages[0]]
        for step in range(1, owners):
            kept.append(lax.ppermute(messages[step], "mom", [(i, (i + step) % owners) for i in range(owners)]))
        return kept, [trade(message[1]) for message in kept]

    own_kernel = kernel.reshape(2 * rows, rows)
    other_kernel = trade(own_kernel)
    packed = pack_fronts(source.reshape(2, rows, columns), dinv.reshape(2 * rows // LANES, LANES), owners)
    traded = [exchange(packed[chunk * owners : (chunk + 1) * owners]) for chunk in range(chunks)]
    front_a, front_b, factors = unpack_fronts(*traded[0], rows, True)
    fronts = [(front_a, front_b)] + [unpack_fronts(*traded[chunk], rows, False) for chunk in range(1, chunks)]
    kernels = hold(own_kernel, other_kernel)
    forward, backward, weights = star_tables(rotation, star_of)

    incoming = [front_a] * DELAY
    before = (front_a, front_b)
    solved, chunked = [], []
    for time in range(items + DELAY * (stages - 1)):
        starting = {}
        for stage in range(stages):
            item = time - DELAY * stage
            if 0 <= item < items and item % SECTIONS == 0:
                starting[item // SECTIONS] = fronts[item // SECTIONS]
        before = tick(time, kernels, factors, starting, incoming[time], before, items)
        solved.append(before)
        incoming.append(onward(before[1]))
        last = time - DELAY * (stages - 1)
        if last >= 0 and last % SECTIONS == SECTIONS - 1:
            candidates = []
            for stage in range(stages):
                candidates.extend(solved[last + DELAY * stage])
            chunked.append(exchange(star_stage(candidates, forward, backward, weights, owners)))
    return assemble(chunked, columns).reshape(1, 2, rows, 1, columns)


def solution(mesh):
    in_specs = (
        P("tm", None, None, None),
        P("tm", None, None, "mom"),
        P("tm", None, None, "mom", None),
        P(),
        P(),
    )
    out_specs = P("tm", None, None, "mom", None)
    return jax.shard_map(shards, mesh=mesh, in_specs=in_specs, out_specs=out_specs, check_vma=False)
```

```python
import functools

import jax
import jax.numpy as jnp
from jax import lax
from jax.experimental import pallas as pl
from jax.experimental.pallas import tpu as pltpu
from jax.sharding import PartitionSpec as P

SECTIONS = 3
LANES = 128
HALF = LANES // 2
DELAY = 2

VMEM = pl.BlockSpec(memory_space=pltpu.VMEM)
ANY = pl.BlockSpec(memory_space=pl.ANY)
F32 = jnp.float32
BF16 = jnp.bfloat16


PARAMS = pltpu.CompilerParams(vmem_limit_bytes=16 * 2**20)


def cost(flops, moved):
    return pl.CostEstimate(flops=flops, bytes_accessed=moved, transcendentals=0)


def lane_index(shape):
    return lax.broadcasted_iota(jnp.int32, shape, len(shape) - 1)


def turn(x, shift, half=HALF):
    shift %= half
    if shift == 0:
        return x
    inside = lax.rem(lane_index(x.shape), half) >= shift
    return jnp.where(inside, pltpu.roll(x, shift, 1), pltpu.roll(x, shift + half, 1))


def lane_block(shape, owners):
    return lax.rem(lane_index(shape), HALF) // (HALF // owners)


def wrap(x, owners):
    return lax.rem(x + 2 * owners, owners)


def to_messages(blocks, owners, place, store):
    width = HALF // owners
    turned = [turn(block, width * q) for q, block in enumerate(blocks)]
    lanes = lane_block(blocks[0].shape, owners)
    for step in range(owners):
        panel = wrap(lanes - place - step, owners)
        message = turned[0]
        for q in range(1, owners):
            message = jnp.where(panel == q, turned[q], message)
        store(step, message.astype(BF16))


def from_messages(messages, owners, place):
    width = HALF // owners
    turned = [turn(message.astype(F32), width * ((owners - step) % owners)) for step, message in enumerate(messages)]
    lanes = lane_block(messages[0].shape, owners)
    panels = []
    for q in range(owners):
        step_of = wrap(place - lanes + q, owners)
        panel = turned[0]
        for step in range(1, owners):
            panel = jnp.where(step_of == step, turned[step], panel)
        panels.append(turn(panel, HALF - width * q))
    return panels


def pack_fronts(source, chunk, owners, dinv=None, own_kernel=None, after=()):
    rows, columns = source.shape[1:]
    panel = rows // owners
    leading = dinv is not None
    extra = 3 * dinv.shape[0] if leading else 0

    def body(source_ref, *refs):
        core = lax.rem(lax.axis_index("tm"), 2)
        place = lax.axis_index("mom")
        low = lane_index((panel, LANES)) < HALF
        out_refs = refs[2:] if leading else refs[len(after) :]
        if leading:
            dinv_ref, own_ref, hold_ref, sem = refs[0], refs[1], refs[2 + owners], refs[3 + owners]
            load = pltpu.make_async_copy(own_ref, hold_ref.at[0], sem)
            load.start()
            first = dinv_ref[...].astype(BF16)
            rest = dinv_ref[...] - first.astype(F32)
            second = rest.astype(BF16)
            third = (rest - second.astype(F32)).astype(BF16)
            pieces = jnp.concatenate([first, second, third])
        for slot in range(2):
            half = core if slot == 0 else 1 - core
            start = pl.multiple_of(half * (columns // 2) + chunk // 2 * LANES, LANES)
            blocks = []
            for q in range(owners):
                real = source_ref[0, pl.ds(q * panel, panel), pl.ds(start, LANES)].astype(F32)
                imag = source_ref[1, pl.ds(q * panel, panel), pl.ds(start, LANES)].astype(F32)
                if chunk % 2 == 0:
                    blocks.append(jnp.where(low, real, pltpu.roll(imag, HALF, 1)))
                else:
                    blocks.append(jnp.where(low, pltpu.roll(real, HALF, 1), imag))

            def store(step, message):
                out_refs[step][slot, pl.ds(0, panel), :] = message

            to_messages(blocks, owners, place, store)
            if leading:
                for step in range(owners):
                    out_refs[step][slot, pl.ds(panel, extra), :] = pieces
        if leading:
            load.wait()

    shapes = [jax.ShapeDtypeStruct((2, panel + extra, LANES), BF16)] * owners
    if leading:
        shapes.append(pltpu.VMEM((2,) + own_kernel.shape, own_kernel.dtype))
    given = (dinv, own_kernel) if leading else tuple(after)
    return pl.pallas_call(
        body,
        out_shape=tuple(shapes),
        in_specs=[VMEM] + ([VMEM, ANY] if leading else [ANY] * len(after)),
        out_specs=(VMEM,) * len(shapes),
        scratch_shapes=[pltpu.SemaphoreType.DMA] if leading else [],
        compiler_params=PARAMS,
        cost_estimate=cost(0, 2 * rows * columns * 2),
        name="pack",
    )(source, *given)


def stack_other(kept, after):
    owners = len(kept)

    def body(*refs):
        for step in range(owners):
            refs[-1][step] = refs[step][1]

    return pl.pallas_call(
        body,
        out_shape=jax.ShapeDtypeStruct((owners,) + kept[0].shape[1:], BF16),
        in_specs=[VMEM] * owners + [ANY] * len(after),
        out_specs=VMEM,
        compiler_params=PARAMS,
        cost_estimate=cost(0, 2 * kept[0].size * owners),
        name="stack",
    )(*kept, *after)


def unpack_fronts(kept, got, rows, kernels=None, other_kernel=None):
    owners = len(kept)
    panel = rows // owners
    blocks = rows // LANES
    extra = kept[0].shape[1] - panel
    leading = kernels is not None

    def body(*refs):
        kept_refs, got_ref = refs[:owners], refs[owners]
        place = lax.axis_index("mom")
        if leading:
            other_ref, outs, hold_ref, sem = refs[owners + 2], refs[owners + 3 : owners + 6], refs[owners + 6], refs[owners + 7]
            load = pltpu.make_async_copy(other_ref, hold_ref.at[1], sem)
            load.start()
        else:
            outs = refs[owners + 1 :]
        for tile in range(2):
            read = (lambda step, span: kept_refs[step][0, span, :]) if tile == 0 else (lambda step, span: got_ref[step, span, :])
            panels = from_messages([read(step, pl.ds(0, panel)) for step in range(owners)], owners, place)
            for q in range(owners):
                outs[tile][pl.ds(q * panel, panel), :] = panels[q].astype(BF16)
            if not leading:
                continue
            pieces = jnp.concatenate([read(step, pl.ds(panel, extra)) for step in range(owners)])
            shape = (owners * extra, LANES)
            row = lax.broadcasted_iota(jnp.int32, shape, 0)
            owner = wrap(place - row // extra, owners)
            wanted = owner == lane_block(shape, owners)
            inner = lax.rem(lax.rem(row, extra), 2 * blocks)
            sign = jnp.where(lane_index(shape) < HALF, -1.0, 1.0)
            for part in range(2):
                scale = jnp.ones(shape, F32) if part == 0 else sign
                for block in range(blocks):
                    pick = jnp.where(wanted & (inner == part * blocks + block), scale, 0.0).astype(BF16)
                    spread = lax.dot_general(pieces, pick, (((0,), (0,)), ((), ())), preferred_element_type=F32)
                    outs[2][tile, part, pl.ds(block * LANES, LANES), :] = spread
        if leading:
            load.wait()

    shapes = [jax.ShapeDtypeStruct((rows, LANES), BF16)] * 2
    given = [*kept, got]
    aliases = {}
    if leading:
        shapes += [pltpu.VMEM((2, 2, rows, LANES), F32), pltpu.VMEM(kernels.shape, kernels.dtype)]
        aliases = {len(given): 3}
        given += [kernels, other_kernel]
    return pl.pallas_call(
        body,
        out_shape=tuple(shapes),
        in_specs=[VMEM] * (owners + 1) + ([VMEM, ANY] if leading else []),
        out_specs=(VMEM,) * len(shapes),
        scratch_shapes=[pltpu.SemaphoreType.DMA] if leading else [],
        input_output_aliases=aliases,
        compiler_params=PARAMS,
        cost_estimate=cost(0, 8 * rows * LANES),
        name="unpack_first" if leading else "unpack_next",
    )(*given)


def tick(time, kernels, factors, fronts, incoming, before, items):
    rows = incoming.shape[0]
    block = min(rows, 512)
    chunks = sorted(fronts)

    def body(kernel_ref, factor_ref, in_ref, *refs):
        front_refs = refs[: 2 * len(chunks)]
        before_a, before_b, out_a, out_b, base_a, base_b = refs[2 * len(chunks) :]
        index = lax.axis_index("tm")
        core = lax.rem(index, 2)
        chip = index // 2
        item = time - DELAY * chip
        section = lax.rem(item + SECTIONS * 64, SECTIONS)
        sign = jnp.where(lane_index((block, LANES)) < HALF, -1.0, 1.0).astype(F32)

        def finish(slot, start, total, target):
            span = pl.ds(start, block)
            turned = pltpu.roll(total, HALF, 1)
            target[span, :] = (factor_ref[slot, 0, span, :] * total + factor_ref[slot, 1, span, :] * turned).astype(BF16)

        def product(slot, start, x_ref):
            real = jnp.dot(kernel_ref[slot, pl.ds(start, block), :], x_ref[...], preferred_element_type=F32)
            imag = jnp.dot(kernel_ref[slot, pl.ds(rows + start, block), :], x_ref[...], preferred_element_type=F32)
            return real + pltpu.roll(imag, HALF, 1) * sign

        @pl.when((item >= 0) & (item < items))
        def _():
            for place, chunk in enumerate(chunks):
                for parity in range(2):

                    @pl.when((item == chunk * SECTIONS) & (core == parity))
                    def _():
                        base_a[...] = front_refs[2 * place + parity][...]
                        base_b[...] = front_refs[2 * place + 1 - parity][...]

            @pl.when(section > 0)
            def _():
                base_a[...] = before_a[...]
                base_b[...] = before_b[...]

            @pl.when(chip == 0)
            def _():
                for start in range(0, rows, block):
                    finish(core, start, base_a[pl.ds(start, block), :].astype(F32), out_a)

            @pl.when(chip > 0)
            def _():
                for start in range(0, rows, block):
                    total = base_a[pl.ds(start, block), :].astype(F32) + product(core, start, in_ref)
                    finish(core, start, total, out_a)

            for start in range(0, rows, block):
                total = base_b[pl.ds(start, block), :].astype(F32) + product(1 - core, start, out_a)
                finish(1 - core, start, total, out_b)

    shape = jax.ShapeDtypeStruct((rows, LANES), BF16)
    given = [front for chunk in chunks for front in fronts[chunk]]
    return pl.pallas_call(
        body,
        out_shape=(shape, shape),
        in_specs=[VMEM] * (5 + len(given)),
        out_specs=(VMEM, VMEM),
        scratch_shapes=[pltpu.VMEM((rows, LANES), BF16)] * 2,
        compiler_params=PARAMS,
        cost_estimate=cost(2 * 4 * rows * rows * 256, 8 * rows * LANES),
        name="tick",
    )(kernels, factors, incoming, *given, *before)


def star_stage(candidates, forward, backward, weights, owners):
    rows = candidates[0].shape[0]
    stages = len(candidates) // 2
    panel = rows // owners
    orbitals = forward.shape[0]
    width = HALF // owners

    def body(*refs):
        inputs = refs[: len(candidates)]
        forward_ref, backward_ref, weight_ref = refs[len(candidates) : len(candidates) + 3]
        out_refs = refs[len(candidates) + 3 : len(candidates) + 3 + owners]
        green_ref, sems = refs[len(candidates) + 3 + owners :]
        index = lax.axis_index("tm")
        core = lax.rem(index, 2)
        chip = index // 2
        place = lax.axis_index("mom")
        for stage in range(stages):
            for parity in range(2):

                @pl.when((chip == stage) & (core == parity))
                def _():
                    copies = [
                        pltpu.make_async_copy(inputs[2 * stage + (parity + slot) % 2], green_ref.at[slot], sems.at[slot])
                        for slot in range(2)
                    ]
                    for copy in copies:
                        copy.start()
                    for copy in copies:
                        copy.wait()

        def mix(x, table_ref):
            groups = x.reshape(panel // orbitals, orbitals, LANES)
            total = groups * table_ref[0]
            for shift in range(1, orbitals):
                total += pltpu.roll(groups, shift, 1) * table_ref[shift]
            return total.reshape(panel, LANES)

        for slot in range(2):
            blocks = []
            for q in range(owners):
                rotated = mix(green_ref[slot, pl.ds(q * panel, panel), :].astype(F32), forward_ref)
                green = rotated * weight_ref[0, :1]
                for step in range(1, owners):
                    green += turn(rotated, width * step) * weight_ref[step, :1]
                square = green * green
                sigma = (square + pltpu.roll(square, HALF, 1)) * green
                blocks.append(mix(sigma, backward_ref))

            def store(step, message):
                out_refs[step][slot] = message

            to_messages(blocks, owners, place, store)

    shape = jax.ShapeDtypeStruct((2, panel, LANES), BF16)
    return pl.pallas_call(
        body,
        out_shape=(shape,) * owners,
        in_specs=[ANY] * len(candidates) + [VMEM] * 3,
        out_specs=(VMEM,) * owners,
        scratch_shapes=[pltpu.VMEM((2, rows, LANES), BF16), pltpu.SemaphoreType.DMA((2,))],
        compiler_params=PARAMS,
        cost_estimate=cost(0, 16 * rows * LANES),
        name="stars",
    )(*candidates, forward, backward, weights)


def assemble(chunked, columns):
    owners = len(chunked[0][0])
    panel = chunked[0][0][0].shape[1]

    def body(*refs):
        out_ref = refs[-1]
        core = lax.rem(lax.axis_index("tm"), 2)
        place = lax.axis_index("mom")
        low = lane_index((panel, LANES)) < HALF
        for side in range(2):
            half = core if side == 0 else 1 - core
            for pair in range(len(chunked) // 2):
                start = pl.multiple_of(half * (columns // 2) + pair * LANES, LANES)
                both = []
                for chunk in (2 * pair, 2 * pair + 1):
                    base = chunk * (owners + 1)
                    messages = [refs[base + d][0] if side == 0 else refs[base + owners][d] for d in range(owners)]
                    both.append(from_messages(messages, owners, place))
                for q in range(owners):
                    first, second = both[0][q], both[1][q]
                    span = pl.ds(q * panel, panel)
                    out_ref[0, span, pl.ds(start, LANES)] = jnp.where(low, first, pltpu.roll(second, HALF, 1)).astype(BF16)
                    out_ref[1, span, pl.ds(start, LANES)] = jnp.where(low, pltpu.roll(first, HALF, 1), second).astype(BF16)

    given = [message for kept, got in chunked for message in (*kept, got)]
    return pl.pallas_call(
        body,
        out_shape=jax.ShapeDtypeStruct((2, owners * panel, columns), BF16),
        in_specs=[VMEM] * len(given),
        out_specs=VMEM,
        compiler_params=PARAMS,
        cost_estimate=cost(0, 8 * owners * panel * columns),
        name="assemble",
    )(*given)


def star_tables(rotation, star_of):
    points, orbitals = rotation.shape[:2]
    width = HALF // points

    def body(rotation_ref, star_ref, forward_ref, backward_ref, weight_ref):
        shape = (orbitals, LANES)
        point = lane_block(shape, points)
        row = lax.broadcasted_iota(jnp.int32, shape, 0)
        columns = []
        for column in range(orbitals):
            total = jnp.zeros(shape, F32)
            for k in range(points):
                entry = rotation_ref[k].astype(F32)[:, column : column + 1]
                total = jnp.where(point == k, jnp.broadcast_to(entry, shape), total)
            columns.append(total)
        for shift in range(orbitals):
            forward = jnp.zeros(shape, F32)
            backward = jnp.zeros(shape, F32)
            for column in range(orbitals):
                here = lax.rem(row - shift + orbitals, orbitals) == column
                forward = jnp.where(here, columns[column], forward)
                moved = columns[column] if shift == 0 else pltpu.roll(columns[column], shift, 0)
                backward = jnp.where(row == column, moved, backward)
            forward_ref[shift] = forward
            backward_ref[shift] = backward
        star = jnp.zeros(shape, F32)
        for k in range(points):
            star = jnp.where(point == k, star_ref[k].astype(F32), star)
        same = [jnp.where(star == turn(star, width * step), 1.0, 0.0) for step in range(points)]
        count = functools.reduce(jnp.add, same)
        for step in range(points):
            weight_ref[step] = same[step] / count

    return pl.pallas_call(
        body,
        out_shape=(
            jax.ShapeDtypeStruct((orbitals, orbitals, LANES), F32),
            jax.ShapeDtypeStruct((orbitals, orbitals, LANES), F32),
            jax.ShapeDtypeStruct((points, orbitals, LANES), F32),
        ),
        in_specs=[VMEM, pl.BlockSpec(memory_space=pltpu.SMEM)],
        out_specs=(VMEM,) * 3,
        compiler_params=PARAMS,
        cost_estimate=cost(0, 12 * orbitals * orbitals * LANES),
        name="tables",
    )(rotation, star_of)


def shards(kernel, dinv, source, rotation, star_of):
    tiles = lax.axis_size("tm")
    owners = lax.axis_size("mom")
    rows = source.shape[2]
    columns = source.shape[4]
    stages = tiles // 2
    chunks = columns // LANES
    items = chunks * SECTIONS
    trade = functools.partial(lax.ppermute, axis_name="tm", perm=[(i, i ^ 1) for i in range(tiles)])
    onward = functools.partial(lax.ppermute, axis_name="tm", perm=[(i, i + 2) for i in range(tiles - 2)])

    def deliver(messages):
        kept = [messages[0]]
        for step in range(1, owners):
            kept.append(lax.ppermute(messages[step], "mom", [(i, (i + step) % owners) for i in range(owners)]))
        return kept

    def exchange(messages):
        kept = deliver(messages)
        return kept, trade(jnp.stack([message[1] for message in kept]))

    own_kernel = kernel.reshape(2 * rows, rows)
    other_kernel = trade(own_kernel)
    planes = source.reshape(2, rows, columns)
    *packed, kernels = pack_fronts(planes, 0, owners, dinv.reshape(2 * rows // LANES, LANES), own_kernel)
    kept, got = exchange(packed)
    front_a, front_b, factors, kernels = unpack_fronts(kept, got, rows, kernels, other_kernel)
    fronts = [(front_a, front_b)]
    forward, backward, weights = star_tables(rotation, star_of)

    incoming = [front_a] * DELAY
    before = (front_a, front_b)
    solved, chunked = [], []
    for time in range(items + DELAY * (stages - 1)):
        starting = {}
        for stage in range(stages):
            item = time - DELAY * stage
            if 0 <= item < items and item % SECTIONS == 0:
                starting[item // SECTIONS] = fronts[item // SECTIONS]
        before = tick(time, kernels, factors, starting, incoming[time], before, items)
        solved.append(before)
        incoming.append(onward(before[1]))
        chunk = time // SECTIONS + 1
        if chunk < chunks and time % SECTIONS == 0:
            kept = deliver(pack_fronts(planes, chunk, owners, after=before[1:]))
        if chunk < chunks and time % SECTIONS == SECTIONS - 1:
            fronts.append(unpack_fronts(kept, trade(stack_other(kept, (before[1], incoming[time + 1]))), rows))
        last = time - DELAY * (stages - 1)
        if last >= 0 and last % SECTIONS == SECTIONS - 1:
            candidates = []
            for stage in range(stages):
                candidates.extend(solved[last + DELAY * stage])
            chunked.append(exchange(star_stage(candidates, forward, backward, weights, owners)))
    return assemble(chunked, columns).reshape(1, 2, rows, 1, columns)


def solution(mesh):
    in_specs = (
        P("tm", None, None, None),
        P("tm", None, None, "mom"),
        P("tm", None, None, "mom", None),
        P(),
        P(),
    )
    out_specs = P("tm", None, None, "mom", None)
    return jax.shard_map(shards, mesh=mesh, in_specs=in_specs, out_specs=out_specs, check_vma=False)
```

```python
import functools

import jax
import jax.numpy as jnp
from jax import lax
from jax.experimental import pallas as pl
from jax.experimental.pallas import tpu as pltpu
from jax.sharding import PartitionSpec as P

SECTIONS = 3
LANES = 128
HALF = LANES // 2
DELAY = 2

VMEM = pl.BlockSpec(memory_space=pltpu.VMEM)
ANY = pl.BlockSpec(memory_space=pl.ANY)
F32 = jnp.float32
BF16 = jnp.bfloat16


PARAMS = pltpu.CompilerParams(vmem_limit_bytes=16 * 2**20)


def cost(flops, moved):
    return pl.CostEstimate(flops=flops, bytes_accessed=moved, transcendentals=0)


def lane_index(shape):
    return lax.broadcasted_iota(jnp.int32, shape, len(shape) - 1)


def turn(x, shift, half=HALF):
    shift %= half
    if shift == 0:
        return x
    inside = lax.rem(lane_index(x.shape), half) >= shift
    return jnp.where(inside, pltpu.roll(x, shift, 1), pltpu.roll(x, shift + half, 1))


def lane_block(shape, owners):
    return lax.rem(lane_index(shape), HALF) // (HALF // owners)


def wrap(x, owners):
    return lax.rem(x + 2 * owners, owners)


def to_messages(blocks, owners, place, store):
    width = HALF // owners
    turned = [turn(block, width * q) for q, block in enumerate(blocks)]
    lanes = lane_block(blocks[0].shape, owners)
    for step in range(owners):
        panel = wrap(lanes - place - step, owners)
        message = turned[0]
        for q in range(1, owners):
            message = jnp.where(panel == q, turned[q], message)
        store(step, message.astype(BF16))


def from_messages(messages, owners, place):
    width = HALF // owners
    turned = [turn(message.astype(F32), width * ((owners - step) % owners)) for step, message in enumerate(messages)]
    lanes = lane_block(messages[0].shape, owners)
    panels = []
    for q in range(owners):
        step_of = wrap(place - lanes + q, owners)
        panel = turned[0]
        for step in range(1, owners):
            panel = jnp.where(step_of == step, turned[step], panel)
        panels.append(turn(panel, HALF - width * q))
    return panels


def pack_fronts(source, chunk, owners, dinv=None, own_kernel=None, after=()):
    rows, columns = source.shape[1:]
    panel = rows // owners
    leading = dinv is not None
    extra = 3 * dinv.shape[0] if leading else 0

    def body(source_ref, *refs):
        core = lax.rem(lax.axis_index("tm"), 2)
        place = lax.axis_index("mom")
        low = lane_index((panel, LANES)) < HALF
        out_refs = refs[2:] if leading else refs[len(after) :]
        if leading:
            dinv_hbm, own_ref, hold_ref, plane_hbm = refs[0], refs[1], refs[2 + owners], source_ref
            source_ref, dinv_ref, sems = refs[3 + owners :]
            loads = [
                pltpu.make_async_copy(dinv_hbm, dinv_ref, sems.at[0]),
                pltpu.make_async_copy(plane_hbm, source_ref, sems.at[1]),
                pltpu.make_async_copy(own_ref, hold_ref.at[0], sems.at[2]),
            ]
            for load in loads:
                load.start()
            loads[0].wait()
            loads[1].wait()
            first = dinv_ref[...].astype(BF16)
            rest = dinv_ref[...] - first.astype(F32)
            second = rest.astype(BF16)
            third = (rest - second.astype(F32)).astype(BF16)
            pieces = jnp.concatenate([first, second, third])
        for slot in range(2):
            half = core if slot == 0 else 1 - core
            start = pl.multiple_of(half * (columns // 2) + chunk // 2 * LANES, LANES)
            blocks = []
            for q in range(owners):
                real = source_ref[0, pl.ds(q * panel, panel), pl.ds(start, LANES)].astype(F32)
                imag = source_ref[1, pl.ds(q * panel, panel), pl.ds(start, LANES)].astype(F32)
                if chunk % 2 == 0:
                    blocks.append(jnp.where(low, real, pltpu.roll(imag, HALF, 1)))
                else:
                    blocks.append(jnp.where(low, pltpu.roll(real, HALF, 1), imag))

            def store(step, message):
                out_refs[step][slot, pl.ds(0, panel), :] = message

            to_messages(blocks, owners, place, store)
            if leading:
                for step in range(owners):
                    out_refs[step][slot, pl.ds(panel, extra), :] = pieces
        if leading:
            loads[2].wait()

    shapes = [jax.ShapeDtypeStruct((2, panel + extra, LANES), BF16)] * owners
    scratch = []
    if leading:
        scratch = [pltpu.VMEM(source.shape, BF16), pltpu.VMEM(dinv.shape, F32), pltpu.SemaphoreType.DMA((3,))]
    if leading:
        shapes.append(pltpu.VMEM((2,) + own_kernel.shape, own_kernel.dtype))
    given = (dinv, own_kernel) if leading else tuple(after)
    return pl.pallas_call(
        body,
        out_shape=tuple(shapes),
        in_specs=[ANY] * 3 if leading else [VMEM] + [ANY] * len(after),
        out_specs=(VMEM,) * len(shapes),
        scratch_shapes=scratch,
        compiler_params=PARAMS,
        cost_estimate=cost(0, 2 * rows * columns * 2),
        name="pack",
    )(source, *given)


def stack_other(kept, after):
    owners = len(kept)

    def body(*refs):
        for step in range(owners):
            refs[-1][step] = refs[step][1]

    return pl.pallas_call(
        body,
        out_shape=jax.ShapeDtypeStruct((owners,) + kept[0].shape[1:], BF16),
        in_specs=[VMEM] * owners + [ANY] * len(after),
        out_specs=VMEM,
        compiler_params=PARAMS,
        cost_estimate=cost(0, 2 * kept[0].size * owners),
        name="stack",
    )(*kept, *after)


def unpack_fronts(kept, got, rows, kernels=None, other_kernel=None):
    owners = len(kept)
    panel = rows // owners
    blocks = rows // LANES
    extra = kept[0].shape[1] - panel
    leading = kernels is not None

    def body(*refs):
        kept_refs, got_ref = refs[:owners], refs[owners]
        place = lax.axis_index("mom")
        if leading:
            other_ref, outs, hold_ref, sem = refs[owners + 2], refs[owners + 3 : owners + 6], refs[owners + 6], refs[owners + 7]
            load = pltpu.make_async_copy(other_ref, hold_ref.at[1], sem)
            load.start()
        else:
            outs = refs[owners + 1 :]
        for tile in range(2):
            read = (lambda step, span: kept_refs[step][0, span, :]) if tile == 0 else (lambda step, span: got_ref[step, span, :])
            panels = from_messages([read(step, pl.ds(0, panel)) for step in range(owners)], owners, place)
            for q in range(owners):
                outs[tile][pl.ds(q * panel, panel), :] = panels[q].astype(BF16)
            if not leading:
                continue
            pieces = jnp.concatenate([read(step, pl.ds(panel, extra)) for step in range(owners)])
            shape = (owners * extra, LANES)
            row = lax.broadcasted_iota(jnp.int32, shape, 0)
            owner = wrap(place - row // extra, owners)
            wanted = owner == lane_block(shape, owners)
            inner = lax.rem(lax.rem(row, extra), 2 * blocks)
            sign = jnp.where(lane_index(shape) < HALF, -1.0, 1.0)
            for part in range(2):
                scale = jnp.ones(shape, F32) if part == 0 else sign
                for block in range(blocks):
                    pick = jnp.where(wanted & (inner == part * blocks + block), scale, 0.0).astype(BF16)
                    spread = lax.dot_general(pieces, pick, (((0,), (0,)), ((), ())), preferred_element_type=F32)
                    outs[2][tile, part, pl.ds(block * LANES, LANES), :] = spread
        if leading:
            load.wait()

    shapes = [jax.ShapeDtypeStruct((rows, LANES), BF16)] * 2
    given = [*kept, got]
    aliases = {}
    if leading:
        shapes += [pltpu.VMEM((2, 2, rows, LANES), F32), pltpu.VMEM(kernels.shape, kernels.dtype)]
        aliases = {len(given): 3}
        given += [kernels, other_kernel]
    return pl.pallas_call(
        body,
        out_shape=tuple(shapes),
        in_specs=[VMEM] * (owners + 1) + ([VMEM, ANY] if leading else []),
        out_specs=(VMEM,) * len(shapes),
        scratch_shapes=[pltpu.SemaphoreType.DMA] if leading else [],
        input_output_aliases=aliases,
        compiler_params=PARAMS,
        cost_estimate=cost(0, 8 * rows * LANES),
        name="unpack_first" if leading else "unpack_next",
    )(*given)


def tick(time, kernels, factors, fronts, incoming, before, items, after):
    rows = incoming.shape[0]
    block = min(rows, 512)
    chunks = sorted(fronts)

    def body(kernel_ref, factor_ref, in_ref, *refs):
        front_refs = refs[: 2 * len(chunks)]
        before_a, before_b, out_a, out_b, base_a, base_b = refs[2 * len(chunks) :][:2] + refs[-4:]
        index = lax.axis_index("tm")
        core = lax.rem(index, 2)
        chip = index // 2
        item = time - DELAY * chip
        section = lax.rem(item + SECTIONS * 64, SECTIONS)
        sign = jnp.where(lane_index((block, LANES)) < HALF, -1.0, 1.0).astype(F32)

        def finish(slot, start, total, target):
            span = pl.ds(start, block)
            turned = pltpu.roll(total, HALF, 1)
            target[span, :] = (factor_ref[slot, 0, span, :] * total + factor_ref[slot, 1, span, :] * turned).astype(BF16)

        def product(slot, start, x_ref):
            real = jnp.dot(kernel_ref[slot, pl.ds(start, block), :], x_ref[...], preferred_element_type=F32)
            imag = jnp.dot(kernel_ref[slot, pl.ds(rows + start, block), :], x_ref[...], preferred_element_type=F32)
            return real + pltpu.roll(imag, HALF, 1) * sign

        @pl.when((item >= 0) & (item < items))
        def _():
            for place, chunk in enumerate(chunks):
                for parity in range(2):

                    @pl.when((item == chunk * SECTIONS) & (core == parity))
                    def _():
                        base_a[...] = front_refs[2 * place + parity][...]
                        base_b[...] = front_refs[2 * place + 1 - parity][...]

            @pl.when(section > 0)
            def _():
                base_a[...] = before_a[...]
                base_b[...] = before_b[...]

            @pl.when(chip == 0)
            def _():
                for start in range(0, rows, block):
                    finish(core, start, base_a[pl.ds(start, block), :].astype(F32), out_a)

            @pl.when(chip > 0)
            def _():
                for start in range(0, rows, block):
                    total = base_a[pl.ds(start, block), :].astype(F32) + product(core, start, in_ref)
                    finish(core, start, total, out_a)

            for start in range(0, rows, block):
                total = base_b[pl.ds(start, block), :].astype(F32) + product(1 - core, start, out_a)
                finish(1 - core, start, total, out_b)

    shape = jax.ShapeDtypeStruct((rows, LANES), BF16)
    given = [front for chunk in chunks for front in fronts[chunk]]
    return pl.pallas_call(
        body,
        out_shape=(shape, shape),
        in_specs=[VMEM] * (5 + len(given)) + [ANY] * len(after),
        out_specs=(VMEM, VMEM),
        scratch_shapes=[pltpu.VMEM((rows, LANES), BF16)] * 2,
        compiler_params=PARAMS,
        cost_estimate=cost(2 * rows * rows * 64, rows * LANES),
        name="tick",
    )(kernels, factors, incoming, *given, *before, *after)


def star_stage(candidates, forward, backward, weights, owners):
    rows = candidates[0].shape[0]
    stages = len(candidates) // 2
    panel = rows // owners
    width = HALF // owners

    def body(*refs):
        inputs = refs[: len(candidates)]
        forward_ref, backward_ref, weight_ref = refs[len(candidates) : len(candidates) + 3]
        out_refs = refs[len(candidates) + 3 : len(candidates) + 3 + owners]
        green_ref, sems = refs[len(candidates) + 3 + owners :]
        index = lax.axis_index("tm")
        core = lax.rem(index, 2)
        chip = index // 2
        place = lax.axis_index("mom")
        for stage in range(stages):
            for parity in range(2):

                @pl.when((chip == stage) & (core == parity))
                def _():
                    copies = [
                        pltpu.make_async_copy(inputs[2 * stage + (parity + slot) % 2], green_ref.at[slot], sems.at[slot])
                        for slot in range(2)
                    ]
                    for copy in copies:
                        copy.start()
                    for copy in copies:
                        copy.wait()

        lanes = lane_block((1, LANES), owners)
        masks = [jnp.where(lanes == k, 1.0, 0.0).astype(BF16) for k in range(owners)]

        def mix(x, table_ref):
            spread = jnp.concatenate([x * mask for mask in masks])
            return jnp.dot(table_ref[...], spread, preferred_element_type=F32)

        for slot in range(2):
            blocks = []
            for q in range(owners):
                parts = []
                for start in range(q * panel, (q + 1) * panel, LANES):
                    rotated = mix(green_ref[slot, pl.ds(start, LANES), :], forward_ref)
                    green = rotated * weight_ref[0, :1]
                    for step in range(1, owners):
                        green += turn(rotated, width * step) * weight_ref[step, :1]
                    square = green * green
                    sigma = (square + pltpu.roll(square, HALF, 1)) * green
                    high = sigma.astype(BF16)
                    low = (sigma - high.astype(F32)).astype(BF16)
                    parts.append(mix(high, backward_ref) + mix(low, backward_ref))
                blocks.append(jnp.concatenate(parts))

            def store(step, message):
                out_refs[step][slot] = message

            to_messages(blocks, owners, place, store)

    shape = jax.ShapeDtypeStruct((2, panel, LANES), BF16)
    return pl.pallas_call(
        body,
        out_shape=(shape,) * owners,
        in_specs=[ANY] * len(candidates) + [VMEM] * 3,
        out_specs=(VMEM,) * owners,
        scratch_shapes=[pltpu.VMEM((2, rows, LANES), BF16), pltpu.SemaphoreType.DMA((2,))],
        compiler_params=PARAMS,
        cost_estimate=cost(0, 16 * rows * LANES),
        name="stars",
    )(*candidates, forward, backward, weights)


def restore(kept, got):
    owners = len(kept)
    panel = kept[0].shape[1]

    def body(*refs):
        place = lax.axis_index("mom")
        for side in range(2):
            messages = [refs[d][0] if side == 0 else refs[owners][d] for d in range(owners)]
            for q, block in enumerate(from_messages(messages, owners, place)):
                refs[-1][side, pl.ds(q * panel, panel), :] = block.astype(BF16)

    return pl.pallas_call(
        body,
        out_shape=jax.ShapeDtypeStruct((2, owners * panel, LANES), BF16),
        in_specs=[VMEM] * (owners + 1),
        out_specs=VMEM,
        compiler_params=PARAMS,
        cost_estimate=cost(0, 8 * owners * panel * LANES),
        name="restore",
    )(*kept, got)


def assemble(restored, kept, got, columns):
    owners = len(kept)
    panel = kept[0].shape[1]
    count = len(restored)

    def body(*refs):
        out_ref = refs[-1]
        core = lax.rem(lax.axis_index("tm"), 2)
        place = lax.axis_index("mom")
        low = lane_index((panel, LANES)) < HALF
        for side in range(2):
            half = core if side == 0 else 1 - core
            messages = [refs[count + d][0] if side == 0 else refs[count + owners][d] for d in range(owners)]
            last = from_messages(messages, owners, place)
            for pair in range((count + 1) // 2):
                start = pl.multiple_of(half * (columns // 2) + pair * LANES, LANES)
                for q in range(owners):
                    span = pl.ds(q * panel, panel)
                    first = refs[2 * pair][side, span, :].astype(F32)
                    second = last[q] if 2 * pair + 1 == count else refs[2 * pair + 1][side, span, :].astype(F32)
                    out_ref[0, span, pl.ds(start, LANES)] = jnp.where(low, first, pltpu.roll(second, HALF, 1)).astype(BF16)
                    out_ref[1, span, pl.ds(start, LANES)] = jnp.where(low, pltpu.roll(first, HALF, 1), second).astype(BF16)

    given = [*restored, *kept, got]
    return pl.pallas_call(
        body,
        out_shape=jax.ShapeDtypeStruct((2, owners * panel, columns), BF16),
        in_specs=[VMEM] * len(given),
        out_specs=VMEM,
        compiler_params=PARAMS,
        cost_estimate=cost(0, 8 * owners * panel * columns),
        name="assemble",
    )(*given)


def star_tables(rotation, star_of):
    points, orbitals = rotation.shape[:2]
    width = HALF // points

    def body(rotation_ref, star_ref, forward_ref, backward_ref, weight_ref):
        square = (LANES, LANES)
        row = lax.broadcasted_iota(jnp.int32, square, 0)
        near = row // orbitals == lane_index(square) // orbitals
        thin = (LANES, orbitals)
        pick = jnp.where(lax.rem(lax.broadcasted_iota(jnp.int32, thin, 0), orbitals) == lane_index(thin), 1.0, 0.0).astype(BF16)

        def product(x, y, side):
            return lax.dot_general(x, y, (((1,), (side,)), ((), ())), preferred_element_type=F32)

        for k in range(points):
            for target, side in ((forward_ref, 0), (backward_ref, 1)):
                tall = product(pick, rotation_ref[k], side).astype(BF16)
                target[:, pl.ds(k * LANES, LANES)] = jnp.where(near, product(tall, pick, 1), 0.0).astype(BF16)
        shape = (orbitals, LANES)
        point = lane_block(shape, points)
        star = jnp.zeros(shape, F32)
        for k in range(points):
            star = jnp.where(point == k, star_ref[k].astype(F32), star)
        same = [jnp.where(star == turn(star, width * step), 1.0, 0.0) for step in range(points)]
        count = functools.reduce(jnp.add, same)
        for step in range(points):
            weight_ref[step] = same[step] / count

    return pl.pallas_call(
        body,
        out_shape=(
            jax.ShapeDtypeStruct((LANES, points * LANES), BF16),
            jax.ShapeDtypeStruct((LANES, points * LANES), BF16),
            jax.ShapeDtypeStruct((points, orbitals, LANES), F32),
        ),
        in_specs=[VMEM, pl.BlockSpec(memory_space=pltpu.SMEM)],
        out_specs=(VMEM,) * 3,
        compiler_params=PARAMS,
        cost_estimate=cost(0, 12 * orbitals * orbitals * LANES),
        name="tables",
    )(rotation, star_of)


def shards(kernel, dinv, source, rotation, star_of):
    tiles = lax.axis_size("tm")
    owners = lax.axis_size("mom")
    rows = source.shape[2]
    columns = source.shape[4]
    stages = tiles // 2
    chunks = columns // LANES
    items = chunks * SECTIONS
    trade = functools.partial(lax.ppermute, axis_name="tm", perm=[(i, i ^ 1) for i in range(tiles)])
    onward = functools.partial(lax.ppermute, axis_name="tm", perm=[(i, i + 2) for i in range(tiles - 2)])

    def deliver(messages):
        kept = [messages[0]]
        for step in range(1, owners):
            kept.append(lax.ppermute(messages[step], "mom", [(i, (i + step) % owners) for i in range(owners)]))
        return kept

    def exchange(messages):
        kept = deliver(messages)
        return kept, trade(jnp.stack([message[1] for message in kept]))

    own_kernel = kernel.reshape(2 * rows, rows)
    other_kernel = trade(own_kernel)
    planes = source.reshape(2, rows, columns)
    stay = functools.partial(pltpu.with_memory_space_constraint, memory_space=pltpu.HBM)
    *packed, kernels = pack_fronts(stay(planes), 0, owners, stay(dinv.reshape(2 * rows // LANES, LANES)), stay(own_kernel))
    kept, got = exchange(packed)
    front_a, front_b, factors, kernels = unpack_fronts(kept, got, rows, kernels, other_kernel)
    fronts = [(front_a, front_b)]
    tables = star_tables(rotation, star_of)
    kept = deliver(pack_fronts(planes, 1, owners, after=(*kept[1:], tables[0])))

    incoming = [front_a] * DELAY
    before = (front_a, front_b)
    solved, chunked = [], []
    for time in range(items + DELAY * (stages - 1)):
        starting = {}
        for stage in range(stages):
            item = time - DELAY * stage
            if 0 <= item < items and item % SECTIONS == 0:
                starting[item // SECTIONS] = fronts[item // SECTIONS]
        before = tick(time, kernels, factors, starting, incoming[time], before, items, kept[time : time + 1] if 0 < time < SECTIONS else [])
        solved.append(before)
        incoming.append(onward(before[1]))
        chunk = time // SECTIONS + 1
        if 1 < chunk < chunks and time % SECTIONS == 0:
            kept = deliver(pack_fronts(planes, chunk, owners, after=before[1:]))
        if chunk < chunks and time % SECTIONS == SECTIONS - 1:
            fronts.append(unpack_fronts(kept, trade(stack_other(kept, (before[1], incoming[time + 1]))), rows))
        last = time - DELAY * (stages - 1)
        if last >= 0 and last % SECTIONS == SECTIONS - 1:
            candidates = []
            for stage in range(stages):
                candidates.extend(solved[last + DELAY * stage])
            chunked.append(exchange(star_stage(candidates, *tables, owners)))
    restored = [restore(*chunk) for chunk in chunked[:-1]]
    return assemble(restored, *chunked[-1], columns).reshape(1, 2, rows, 1, columns)


def solution(mesh):
    in_specs = (
        P("tm", None, None, None),
        P("tm", None, None, "mom"),
        P("tm", None, None, "mom", None),
        P(),
        P(),
    )
    out_specs = P("tm", None, None, "mom", None)
    return jax.shard_map(shards, mesh=mesh, in_specs=in_specs, out_specs=out_specs, check_vma=False)
```

```python
import functools

import jax
import jax.numpy as jnp
from jax import lax
from jax.experimental import pallas as pl
from jax.experimental.pallas import tpu as pltpu
from jax.sharding import PartitionSpec as P

SECTIONS = 3
LANES = 128
HALF = LANES // 2
DELAY = 2
BLOCK = 256

VMEM = pl.BlockSpec(memory_space=pltpu.VMEM)
ANY = pl.BlockSpec(memory_space=pl.ANY)
F32 = jnp.float32
BF16 = jnp.bfloat16


PARAMS = pltpu.CompilerParams(vmem_limit_bytes=16 * 2**20)


def cost(flops, moved):
    return pl.CostEstimate(flops=flops, bytes_accessed=moved, transcendentals=0)


def lane_index(shape):
    return lax.broadcasted_iota(jnp.int32, shape, len(shape) - 1)


def turn(x, shift, half=HALF):
    shift %= half
    if shift == 0:
        return x
    inside = (lane_index(x.shape) & (half - 1)) >= shift
    return jnp.where(inside, pltpu.roll(x, shift, 1), pltpu.roll(x, shift + half, 1))


def lane_block(shape, owners):
    return (lane_index(shape) & (HALF - 1)) >> ((HALF // owners).bit_length() - 1)


def wrap(x, owners):
    return (x + 2 * owners) & (owners - 1)


def to_messages(blocks, owners, place, store):
    width = HALF // owners
    turned = [turn(block, width * q) for q, block in enumerate(blocks)]
    lanes = lane_block(blocks[0].shape, owners)
    for step in range(owners):
        panel = wrap(lanes - place - step, owners)
        message = turned[0]
        for q in range(1, owners):
            message = jnp.where(panel == q, turned[q], message)
        store(step, message.astype(BF16))


def from_messages(messages, owners, place):
    width = HALF // owners
    turned = [turn(message.astype(F32), width * ((owners - step) % owners)) for step, message in enumerate(messages)]
    lanes = lane_block(messages[0].shape, owners)
    panels = []
    for q in range(owners):
        step_of = wrap(place - lanes + q, owners)
        panel = turned[0]
        for step in range(1, owners):
            panel = jnp.where(step_of == step, turned[step], panel)
        panels.append(turn(panel, HALF - width * q))
    return panels


def pack_fronts(source, chunk, owners, dinv=None, own_kernel=None, after=()):
    rows, columns = source.shape[1:]
    panel = rows // owners
    leading = dinv is not None
    extra = 3 * dinv.shape[0] if leading else 0

    def body(source_ref, *refs):
        core = lax.rem(lax.axis_index("tm"), 2)
        place = lax.axis_index("mom")
        low = lane_index((panel, LANES)) < HALF
        out_refs = refs[2:] if leading else refs[len(after) :]
        if leading:
            dinv_hbm, own_ref, hold_ref, plane_hbm = refs[0], refs[1], refs[2 + owners], source_ref
            source_ref, dinv_ref, sems = refs[3 + owners :]
            loads = [
                pltpu.make_async_copy(dinv_hbm, dinv_ref, sems.at[0]),
                pltpu.make_async_copy(plane_hbm, source_ref, sems.at[1]),
                pltpu.make_async_copy(own_ref, hold_ref.at[0], sems.at[2]),
            ]
            for load in loads:
                load.start()
            loads[0].wait()
            loads[1].wait()
            first = dinv_ref[...].astype(BF16)
            rest = dinv_ref[...] - first.astype(F32)
            second = rest.astype(BF16)
            third = (rest - second.astype(F32)).astype(BF16)
            pieces = jnp.concatenate([first, second, third])
        for slot in range(2):
            half = core if slot == 0 else 1 - core
            start = pl.multiple_of(half * (columns // 2) + chunk // 2 * LANES, LANES)
            blocks = []
            for q in range(owners):
                real = source_ref[0, pl.ds(q * panel, panel), pl.ds(start, LANES)].astype(F32)
                imag = source_ref[1, pl.ds(q * panel, panel), pl.ds(start, LANES)].astype(F32)
                if chunk % 2 == 0:
                    blocks.append(jnp.where(low, real, pltpu.roll(imag, HALF, 1)))
                else:
                    blocks.append(jnp.where(low, pltpu.roll(real, HALF, 1), imag))

            def store(step, message):
                out_refs[step][slot, pl.ds(0, panel), :] = message

            to_messages(blocks, owners, place, store)
            if leading:
                for step in range(owners):
                    out_refs[step][slot, pl.ds(panel, extra), :] = pieces
        if leading:
            loads[2].wait()

    shapes = [jax.ShapeDtypeStruct((2, panel + extra, LANES), BF16)] * owners
    scratch = []
    if leading:
        scratch = [pltpu.VMEM(source.shape, BF16), pltpu.VMEM(dinv.shape, F32), pltpu.SemaphoreType.DMA((3,))]
    if leading:
        shapes.append(pltpu.VMEM((2,) + own_kernel.shape, own_kernel.dtype))
    given = (dinv, own_kernel) if leading else tuple(after)
    return pl.pallas_call(
        body,
        out_shape=tuple(shapes),
        in_specs=[ANY] * 3 if leading else [VMEM] + [ANY] * len(after),
        out_specs=(VMEM,) * len(shapes),
        scratch_shapes=scratch,
        compiler_params=PARAMS,
        cost_estimate=cost(0, 2 * rows * columns * 2),
        name="pack",
    )(source, *given)


def stack_other(kept, after):
    owners = len(kept)

    def body(*refs):
        for step in range(owners):
            refs[-1][step] = refs[step][1]

    return pl.pallas_call(
        body,
        out_shape=jax.ShapeDtypeStruct((owners,) + kept[0].shape[1:], BF16),
        in_specs=[VMEM] * owners + [ANY] * len(after),
        out_specs=VMEM,
        compiler_params=PARAMS,
        cost_estimate=cost(0, 2 * kept[0].size * owners),
        name="stack",
    )(*kept, *after)


def unpack_fronts(kept, got, rows, kernels=None, other_kernel=None):
    owners = len(kept)
    panel = rows // owners
    blocks = rows // LANES
    extra = kept[0].shape[1] - panel
    leading = kernels is not None

    def body(*refs):
        kept_refs, got_ref = refs[:owners], refs[owners]
        place = lax.axis_index("mom")
        if leading:
            other_ref, outs, hold_ref, sem = refs[owners + 2], refs[owners + 3 : owners + 6], refs[owners + 6], refs[owners + 7]
            load = pltpu.make_async_copy(other_ref, hold_ref.at[1], sem)
            load.start()
        else:
            outs = refs[owners + 1 :]
        for tile in range(2):
            read = (lambda step, span: kept_refs[step][0, span, :]) if tile == 0 else (lambda step, span: got_ref[step, span, :])
            panels = from_messages([read(step, pl.ds(0, panel)) for step in range(owners)], owners, place)
            for q in range(owners):
                outs[tile][pl.ds(q * panel, panel), :] = panels[q].astype(BF16)
            if not leading:
                continue
            pieces = jnp.concatenate([read(step, pl.ds(panel, extra)) for step in range(owners)])
            shape = (owners * extra, LANES)
            row = lax.broadcasted_iota(jnp.int32, shape, 0)
            owner = wrap(place - row // extra, owners)
            wanted = owner == lane_block(shape, owners)
            inner = lax.rem(lax.rem(row, extra), 2 * blocks)
            sign = jnp.where(lane_index(shape) < HALF, -1.0, 1.0)
            for part in range(2):
                scale = jnp.ones(shape, F32) if part == 0 else sign
                for block in range(blocks):
                    pick = jnp.where(wanted & (inner == part * blocks + block), scale, 0.0).astype(BF16)
                    spread = lax.dot_general(pieces, pick, (((0,), (0,)), ((), ())), preferred_element_type=F32)
                    outs[2][tile, part, pl.ds(block * LANES, LANES), :] = spread
        if leading:
            load.wait()

    shapes = [jax.ShapeDtypeStruct((rows, LANES), BF16)] * 2
    given = [*kept, got]
    aliases = {}
    if leading:
        shapes += [pltpu.VMEM((2, 2, rows, LANES), F32), pltpu.VMEM(kernels.shape, kernels.dtype)]
        aliases = {len(given): 3}
        given += [kernels, other_kernel]
    return pl.pallas_call(
        body,
        out_shape=tuple(shapes),
        in_specs=[VMEM] * (owners + 1) + ([VMEM, ANY] if leading else []),
        out_specs=(VMEM,) * len(shapes),
        scratch_shapes=[pltpu.SemaphoreType.DMA] if leading else [],
        input_output_aliases=aliases,
        compiler_params=PARAMS,
        cost_estimate=cost(0, 8 * rows * LANES),
        name="unpack_first" if leading else "unpack_next",
    )(*given)


def tick(time, kernels, factors, fronts, incoming, before, items, after):
    rows = incoming.shape[0]
    block = min(rows, BLOCK)
    chunks = sorted(fronts)

    def body(kernel_ref, factor_ref, in_ref, *refs):
        front_refs = refs[: 2 * len(chunks)]
        before_a, before_b, out_a, out_b, base_a, base_b = refs[2 * len(chunks) :][:2] + refs[-4:]
        index = lax.axis_index("tm")
        core = lax.rem(index, 2)
        chip = index // 2
        item = time - DELAY * chip
        section = lax.rem(item + SECTIONS * 64, SECTIONS)
        sign = jnp.where(lane_index((block, LANES)) < HALF, -1.0, 1.0).astype(F32)

        def finish(slot, start, total, target):
            span = pl.ds(start, block)
            turned = pltpu.roll(total, HALF, 1)
            target[span, :] = (factor_ref[slot, 0, span, :] * total + factor_ref[slot, 1, span, :] * turned).astype(BF16)

        def product(slot, start, x_ref):
            real = jnp.dot(kernel_ref[slot, pl.ds(start, block), :], x_ref[...], preferred_element_type=F32)
            imag = jnp.dot(kernel_ref[slot, pl.ds(rows + start, block), :], x_ref[...], preferred_element_type=F32)
            return real + pltpu.roll(imag, HALF, 1) * sign

        @pl.when((item >= 0) & (item < items))
        def _():
            for place, chunk in enumerate(chunks):
                for parity in range(2):

                    @pl.when((item == chunk * SECTIONS) & (core == parity))
                    def _():
                        base_a[...] = front_refs[2 * place + parity][...]
                        base_b[...] = front_refs[2 * place + 1 - parity][...]

            @pl.when(section > 0)
            def _():
                base_a[...] = before_a[...]
                base_b[...] = before_b[...]

            @pl.when(chip == 0)
            def _():
                for start in range(0, rows, block):
                    finish(core, start, base_a[pl.ds(start, block), :].astype(F32), out_a)

            @pl.when(chip > 0)
            def _():
                for start in range(0, rows, block):
                    total = base_a[pl.ds(start, block), :].astype(F32) + product(core, start, in_ref)
                    finish(core, start, total, out_a)

            for start in range(0, rows, block):
                total = base_b[pl.ds(start, block), :].astype(F32) + product(1 - core, start, out_a)
                finish(1 - core, start, total, out_b)

    shape = jax.ShapeDtypeStruct((rows, LANES), BF16)
    given = [front for chunk in chunks for front in fronts[chunk]]
    return pl.pallas_call(
        body,
        out_shape=(shape, shape),
        in_specs=[VMEM] * (5 + len(given)) + [ANY] * len(after),
        out_specs=(VMEM, VMEM),
        scratch_shapes=[pltpu.VMEM((rows, LANES), BF16)] * 2,
        compiler_params=PARAMS,
        cost_estimate=cost(2 * rows * rows * 64, rows * LANES),
        name="tick",
    )(kernels, factors, incoming, *given, *before, *after)


def star_stage(candidates, forward, backward, weights, owners):
    rows = candidates[0].shape[0]
    stages = len(candidates) // 2
    panel = rows // owners
    orbitals = backward.shape[0]
    width = HALF // owners

    def body(*refs):
        inputs = refs[: len(candidates)]
        forward_ref, backward_ref, weight_ref = refs[len(candidates) : len(candidates) + 3]
        out_refs = refs[len(candidates) + 3 : len(candidates) + 3 + owners]
        green_ref = refs[-1]
        index = lax.axis_index("tm")
        core = lax.rem(index, 2)
        chip = index // 2
        place = lax.axis_index("mom")
        for stage in range(stages):
            for parity in range(2):

                @pl.when((chip == stage) & (core == parity))
                def _():
                    for slot in range(2):
                        green_ref[slot] = inputs[2 * stage + (parity + slot) % 2][...]

        def mix(x, table_ref):
            groups = x.reshape(panel // orbitals, orbitals, LANES)
            total = groups * table_ref[0]
            for shift in range(1, orbitals):
                total += pltpu.roll(groups, shift, 1) * table_ref[shift]
            return total.reshape(panel, LANES)

        for slot in range(2):
            blocks = []
            for q in range(owners):
                rotated = mix(green_ref[slot, pl.ds(q * panel, panel), :].astype(F32), forward_ref)
                green = rotated * weight_ref[0, :1]
                for step in range(1, owners):
                    green += turn(rotated, width * step) * weight_ref[step, :1]
                square = green * green
                sigma = (square + pltpu.roll(square, HALF, 1)) * green
                blocks.append(mix(sigma, backward_ref))

            def store(step, message):
                out_refs[step][slot] = message

            to_messages(blocks, owners, place, store)

    shape = jax.ShapeDtypeStruct((2, panel, LANES), BF16)
    return pl.pallas_call(
        body,
        out_shape=(shape,) * owners,
        in_specs=[VMEM] * (len(candidates) + 3),
        out_specs=(VMEM,) * owners,
        scratch_shapes=[pltpu.VMEM((2, rows, LANES), BF16)],
        compiler_params=PARAMS,
        cost_estimate=cost(0, 16 * rows * LANES),
        name="stars",
    )(*candidates, forward, backward, weights)


def restore(kept, got):
    owners = len(kept)
    panel = kept[0].shape[1]

    def body(*refs):
        place = lax.axis_index("mom")
        for side in range(2):
            messages = [refs[d][0] if side == 0 else refs[owners][d] for d in range(owners)]
            for q, block in enumerate(from_messages(messages, owners, place)):
                refs[-1][side, pl.ds(q * panel, panel), :] = block.astype(BF16)

    return pl.pallas_call(
        body,
        out_shape=jax.ShapeDtypeStruct((2, owners * panel, LANES), BF16),
        in_specs=[VMEM] * (owners + 1),
        out_specs=VMEM,
        compiler_params=PARAMS,
        cost_estimate=cost(0, 8 * owners * panel * LANES),
        name="restore",
    )(*kept, got)


def assemble(restored, kept, got, columns):
    owners = len(kept)
    panel = kept[0].shape[1]
    count = len(restored)

    def body(*refs):
        out_ref = refs[-1]
        core = lax.rem(lax.axis_index("tm"), 2)
        place = lax.axis_index("mom")
        low = lane_index((panel, LANES)) < HALF
        for side in range(2):
            half = core if side == 0 else 1 - core
            messages = [refs[count + d][0] if side == 0 else refs[count + owners][d] for d in range(owners)]
            last = from_messages(messages, owners, place)
            for pair in range((count + 1) // 2):
                start = pl.multiple_of(half * (columns // 2) + pair * LANES, LANES)
                for q in range(owners):
                    span = pl.ds(q * panel, panel)
                    first = refs[2 * pair][side, span, :].astype(F32)
                    second = last[q] if 2 * pair + 1 == count else refs[2 * pair + 1][side, span, :].astype(F32)
                    out_ref[0, span, pl.ds(start, LANES)] = jnp.where(low, first, pltpu.roll(second, HALF, 1)).astype(BF16)
                    out_ref[1, span, pl.ds(start, LANES)] = jnp.where(low, pltpu.roll(first, HALF, 1), second).astype(BF16)

    given = [*restored, *kept, got]
    return pl.pallas_call(
        body,
        out_shape=jax.ShapeDtypeStruct((2, owners * panel, columns), BF16),
        in_specs=[VMEM] * len(given),
        out_specs=VMEM,
        compiler_params=PARAMS,
        cost_estimate=cost(0, 8 * owners * panel * columns),
        name="assemble",
    )(*given)


def star_tables(rotation, star_of):
    points, orbitals = rotation.shape[:2]
    width = HALF // points

    def body(rotation_ref, star_ref, forward_ref, backward_ref, weight_ref):
        shape = (orbitals, LANES)
        point = lane_block(shape, points)
        row = lax.broadcasted_iota(jnp.int32, shape, 0)
        columns = []
        for column in range(orbitals):
            total = jnp.zeros(shape, F32)
            for k in range(points):
                entry = rotation_ref[k].astype(F32)[:, column : column + 1]
                total = jnp.where(point == k, jnp.broadcast_to(entry, shape), total)
            columns.append(total)
        for shift in range(orbitals):
            forward = jnp.zeros(shape, F32)
            backward = jnp.zeros(shape, F32)
            for column in range(orbitals):
                here = lax.rem(row - shift + orbitals, orbitals) == column
                forward = jnp.where(here, columns[column], forward)
                moved = columns[column] if shift == 0 else pltpu.roll(columns[column], shift, 0)
                backward = jnp.where(row == column, moved, backward)
            forward_ref[shift] = forward
            backward_ref[shift] = backward
        star = jnp.zeros(shape, F32)
        for k in range(points):
            star = jnp.where(point == k, star_ref[k].astype(F32), star)
        same = [jnp.where(star == turn(star, width * step), 1.0, 0.0) for step in range(points)]
        count = functools.reduce(jnp.add, same)
        for step in range(points):
            weight_ref[step] = same[step] / count

    return pl.pallas_call(
        body,
        out_shape=(
            jax.ShapeDtypeStruct((orbitals, orbitals, LANES), F32),
            jax.ShapeDtypeStruct((orbitals, orbitals, LANES), F32),
            jax.ShapeDtypeStruct((points, orbitals, LANES), F32),
        ),
        in_specs=[VMEM, pl.BlockSpec(memory_space=pltpu.SMEM)],
        out_specs=(VMEM,) * 3,
        compiler_params=PARAMS,
        cost_estimate=cost(0, 12 * orbitals * orbitals * LANES),
        name="tables",
    )(rotation, star_of)


def shards(kernel, dinv, source, rotation, star_of):
    tiles = lax.axis_size("tm")
    owners = lax.axis_size("mom")
    rows = source.shape[2]
    columns = source.shape[4]
    stages = tiles // 2
    chunks = columns // LANES
    items = chunks * SECTIONS
    trade = functools.partial(lax.ppermute, axis_name="tm", perm=[(i, i ^ 1) for i in range(tiles)])
    onward = functools.partial(lax.ppermute, axis_name="tm", perm=[(i, i + 2) for i in range(tiles - 2)])

    def deliver(messages):
        kept = [messages[0]]
        for step in range(1, owners):
            kept.append(lax.ppermute(messages[step], "mom", [(i, (i + step) % owners) for i in range(owners)]))
        return kept

    own_kernel = kernel.reshape(2 * rows, rows)
    other_kernel = trade(own_kernel)
    planes = source.reshape(2, rows, columns)
    stay = functools.partial(pltpu.with_memory_space_constraint, memory_space=pltpu.HBM)
    *packed, kernels = pack_fronts(stay(planes), 0, owners, stay(dinv.reshape(2 * rows // LANES, LANES)), stay(own_kernel))
    tables = star_tables(rotation, star_of)
    ready = pack_fronts(planes, 1, owners, after=(packed[0], tables[0]))
    kept = deliver(packed)
    got = trade(stack_other(kept, ready[:1]))
    front_a, front_b, factors, kernels = unpack_fronts(kept, got, rows, kernels, other_kernel)
    fronts = [(front_a, front_b)]
    kept = deliver(ready)

    incoming = [front_a] * DELAY
    before = (front_a, front_b)
    solved, chunked = [], []
    for time in range(items + DELAY * (stages - 1)):
        starting = {}
        for stage in range(stages):
            item = time - DELAY * stage
            if 0 <= item < items and item % SECTIONS == 0:
                starting[item // SECTIONS] = fronts[item // SECTIONS]
        before = tick(time, kernels, factors, starting, incoming[time], before, items, kept[time : time + 1] if 0 < time < SECTIONS else [])
        solved.append(before)
        incoming.append(onward(before[1]))
        chunk = time // SECTIONS + 1
        if 1 < chunk < chunks and time % SECTIONS == 0:
            kept = deliver(pack_fronts(planes, chunk, owners, after=before[1:]))
        if chunk < chunks and time % SECTIONS == SECTIONS - 1:
            fronts.append(unpack_fronts(kept, trade(stack_other(kept, (before[1], incoming[time + 1]))), rows))
        last = time - DELAY * (stages - 1)
        if last >= 0 and last % SECTIONS == SECTIONS - 1:
            candidates = []
            for stage in range(stages):
                candidates.extend(solved[last + DELAY * stage])
            chunked.append(deliver(star_stage(candidates, *tables, owners)))
    restored = []
    for back in chunked[:-1]:
        restored.append(restore(back, trade(stack_other(back, ()))))
    back = chunked[-1]
    return assemble(restored, back, trade(stack_other(back, restored)), columns).reshape(1, 2, rows, 1, columns)


def solution(mesh):
    in_specs = (
        P("tm", None, None, None),
        P("tm", None, None, "mom"),
        P("tm", None, None, "mom", None),
        P(),
        P(),
    )
    out_specs = P("tm", None, None, "mom", None)
    return jax.shard_map(shards, mesh=mesh, in_specs=in_specs, out_specs=out_specs, check_vma=False)
```

```python
import functools

import jax
import jax.numpy as jnp
from jax import lax
from jax.experimental import pallas as pl
from jax.experimental.pallas import tpu as pltpu
from jax.sharding import PartitionSpec as P

SECTIONS = 3
LANES = 128
HALF = LANES // 2
DELAY = 2
BLOCK = 256

VMEM = pl.BlockSpec(memory_space=pltpu.VMEM)
ANY = pl.BlockSpec(memory_space=pl.ANY)
F32 = jnp.float32
BF16 = jnp.bfloat16


PARAMS = pltpu.CompilerParams(vmem_limit_bytes=16 * 2**20)


def cost(flops, moved):
    return pl.CostEstimate(flops=flops, bytes_accessed=moved, transcendentals=0)


def lane_index(shape):
    return lax.broadcasted_iota(jnp.int32, shape, len(shape) - 1)


def turn(x, shift, half=HALF):
    shift %= half
    if shift == 0:
        return x
    inside = (lane_index(x.shape) & (half - 1)) >= shift
    return jnp.where(inside, pltpu.roll(x, shift, 1), pltpu.roll(x, shift + half, 1))


def lane_block(shape, owners):
    return (lane_index(shape) & (HALF - 1)) >> ((HALF // owners).bit_length() - 1)


def wrap(x, owners):
    return (x + 2 * owners) & (owners - 1)


def to_messages(blocks, owners, place, store):
    width = HALF // owners
    turned = [turn(block, width * q) for q, block in enumerate(blocks)]
    lanes = lane_block(blocks[0].shape, owners)
    for step in range(owners):
        panel = wrap(lanes - place - step, owners)
        message = turned[0]
        for q in range(1, owners):
            message = jnp.where(panel == q, turned[q], message)
        store(step, message.astype(BF16))


def from_messages(messages, owners, place):
    width = HALF // owners
    turned = [turn(message.astype(F32), width * ((owners - step) % owners)) for step, message in enumerate(messages)]
    lanes = lane_block(messages[0].shape, owners)
    panels = []
    for q in range(owners):
        step_of = wrap(place - lanes + q, owners)
        panel = turned[0]
        for step in range(1, owners):
            panel = jnp.where(step_of == step, turned[step], panel)
        panels.append(turn(panel, HALF - width * q))
    return panels


def pack_fronts(source, chunk, owners, dinv=None, own_kernel=None, after=()):
    rows, columns = source.shape[1:]
    panel = rows // owners
    leading = dinv is not None
    extra = 3 * dinv.shape[0] if leading else 0

    def body(source_ref, *refs):
        core = lax.rem(lax.axis_index("tm"), 2)
        place = lax.axis_index("mom")
        low = lane_index((panel, LANES)) < HALF
        out_refs = refs[2:] if leading else refs[len(after) :]
        if leading:
            dinv_hbm, own_ref, hold_ref, plane_hbm = refs[0], refs[1], refs[2 + owners], source_ref
            source_ref, dinv_ref, sems = refs[3 + owners :]
            loads = [
                pltpu.make_async_copy(dinv_hbm, dinv_ref, sems.at[0]),
                pltpu.make_async_copy(plane_hbm, source_ref, sems.at[1]),
                pltpu.make_async_copy(own_ref, hold_ref.at[0], sems.at[2]),
            ]
            for load in loads:
                load.start()
            loads[0].wait()
            loads[1].wait()
            first = dinv_ref[...].astype(BF16)
            rest = dinv_ref[...] - first.astype(F32)
            second = rest.astype(BF16)
            third = (rest - second.astype(F32)).astype(BF16)
            pieces = jnp.concatenate([first, second, third])
        for slot in range(2):
            half = core if slot == 0 else 1 - core
            start = pl.multiple_of(half * (columns // 2) + chunk // 2 * LANES, LANES)
            blocks = []
            for q in range(owners):
                real = source_ref[0, pl.ds(q * panel, panel), pl.ds(start, LANES)].astype(F32)
                imag = source_ref[1, pl.ds(q * panel, panel), pl.ds(start, LANES)].astype(F32)
                if chunk % 2 == 0:
                    blocks.append(jnp.where(low, real, pltpu.roll(imag, HALF, 1)))
                else:
                    blocks.append(jnp.where(low, pltpu.roll(real, HALF, 1), imag))

            def store(step, message):
                out_refs[step][slot, pl.ds(0, panel), :] = message

            to_messages(blocks, owners, place, store)
            if leading:
                for step in range(owners):
                    out_refs[step][slot, pl.ds(panel, extra), :] = pieces
        if leading:
            loads[2].wait()

    shapes = [jax.ShapeDtypeStruct((2, panel + extra, LANES), BF16)] * owners
    scratch = []
    if leading:
        scratch = [pltpu.VMEM(source.shape, BF16), pltpu.VMEM(dinv.shape, F32), pltpu.SemaphoreType.DMA((3,))]
    if leading:
        shapes.append(pltpu.VMEM((2,) + own_kernel.shape, own_kernel.dtype))
    given = (dinv, own_kernel) if leading else tuple(after)
    return pl.pallas_call(
        body,
        out_shape=tuple(shapes),
        in_specs=[ANY] * 3 if leading else [VMEM] + [ANY] * len(after),
        out_specs=(VMEM,) * len(shapes),
        scratch_shapes=scratch,
        compiler_params=PARAMS,
        cost_estimate=cost(0, 2 * rows * columns * 2),
        name="pack",
    )(source, *given)


def stack_other(kept, after):
    owners = len(kept)

    def body(*refs):
        for step in range(owners):
            refs[-1][step] = refs[step][1]

    return pl.pallas_call(
        body,
        out_shape=jax.ShapeDtypeStruct((owners,) + kept[0].shape[1:], BF16),
        in_specs=[VMEM] * owners + [ANY] * len(after),
        out_specs=VMEM,
        compiler_params=PARAMS,
        cost_estimate=cost(0, 2 * kept[0].size * owners),
        name="stack",
    )(*kept, *after)


def unpack_fronts(kept, got, rows, kernels=None, other_kernel=None):
    owners = len(kept)
    panel = rows // owners
    blocks = rows // LANES
    extra = kept[0].shape[1] - panel
    leading = kernels is not None

    def body(*refs):
        kept_refs, got_ref = refs[:owners], refs[owners]
        place = lax.axis_index("mom")
        if leading:
            other_ref, outs, hold_ref, sem = refs[owners + 2], refs[owners + 3 : owners + 6], refs[owners + 6], refs[owners + 7]
            load = pltpu.make_async_copy(other_ref, hold_ref.at[1], sem)
            load.start()
        else:
            outs = refs[owners + 1 :]
        for tile in range(2):
            read = (lambda step, span: kept_refs[step][0, span, :]) if tile == 0 else (lambda step, span: got_ref[step, span, :])
            panels = from_messages([read(step, pl.ds(0, panel)) for step in range(owners)], owners, place)
            for q in range(owners):
                outs[tile][pl.ds(q * panel, panel), :] = panels[q].astype(BF16)
            if not leading:
                continue
            pieces = jnp.concatenate([read(step, pl.ds(panel, extra)) for step in range(owners)])
            shape = (owners * extra, LANES)
            row = lax.broadcasted_iota(jnp.int32, shape, 0)
            owner = wrap(place - row // extra, owners)
            wanted = owner == lane_block(shape, owners)
            inner = lax.rem(lax.rem(row, extra), 2 * blocks)
            sign = jnp.where(lane_index(shape) < HALF, -1.0, 1.0)
            for part in range(2):
                scale = jnp.ones(shape, F32) if part == 0 else sign
                for block in range(blocks):
                    pick = jnp.where(wanted & (inner == part * blocks + block), scale, 0.0).astype(BF16)
                    spread = lax.dot_general(pieces, pick, (((0,), (0,)), ((), ())), preferred_element_type=F32)
                    outs[2][tile, part, pl.ds(block * LANES, LANES), :] = spread
        if leading:
            load.wait()

    shapes = [jax.ShapeDtypeStruct((rows, LANES), BF16)] * 2
    given = [*kept, got]
    aliases = {}
    if leading:
        shapes += [pltpu.VMEM((2, 2, rows, LANES), F32), pltpu.VMEM(kernels.shape, kernels.dtype)]
        aliases = {len(given): 3}
        given += [kernels, other_kernel]
    return pl.pallas_call(
        body,
        out_shape=tuple(shapes),
        in_specs=[VMEM] * (owners + 1) + ([VMEM, ANY] if leading else []),
        out_specs=(VMEM,) * len(shapes),
        scratch_shapes=[pltpu.SemaphoreType.DMA] if leading else [],
        input_output_aliases=aliases,
        compiler_params=PARAMS,
        cost_estimate=cost(0, 8 * rows * LANES),
        name="unpack_first" if leading else "unpack_next",
    )(*given)


def tick(time, kernels, factors, fronts, incoming, before, items, after):
    rows = incoming.shape[0]
    block = min(rows, BLOCK)
    chunks = sorted(fronts)

    def body(kernel_ref, factor_ref, in_ref, *refs):
        front_refs = refs[: 2 * len(chunks)]
        before_a, before_b, out_a, out_b, base_a, base_b = refs[2 * len(chunks) :][:2] + refs[-4:]
        index = lax.axis_index("tm")
        core = lax.rem(index, 2)
        chip = index // 2
        item = time - DELAY * chip
        section = lax.rem(item + SECTIONS * 64, SECTIONS)
        sign = jnp.where(lane_index((block, LANES)) < HALF, -1.0, 1.0).astype(F32)

        def finish(slot, start, total, target):
            span = pl.ds(start, block)
            turned = pltpu.roll(total, HALF, 1)
            target[span, :] = (factor_ref[slot, 0, span, :] * total + factor_ref[slot, 1, span, :] * turned).astype(BF16)

        def product(slot, start, x_ref):
            real = jnp.dot(kernel_ref[slot, pl.ds(start, block), :], x_ref[...], preferred_element_type=F32)
            imag = jnp.dot(kernel_ref[slot, pl.ds(rows + start, block), :], x_ref[...], preferred_element_type=F32)
            return real + pltpu.roll(imag, HALF, 1) * sign

        @pl.when((item >= 0) & (item < items))
        def _():
            for place, chunk in enumerate(chunks):
                for parity in range(2):

                    @pl.when((item == chunk * SECTIONS) & (core == parity))
                    def _():
                        base_a[...] = front_refs[2 * place + parity][...]
                        base_b[...] = front_refs[2 * place + 1 - parity][...]

            @pl.when(section > 0)
            def _():
                base_a[...] = before_a[...]
                base_b[...] = before_b[...]

            @pl.when(chip == 0)
            def _():
                for start in range(0, rows, block):
                    finish(core, start, base_a[pl.ds(start, block), :].astype(F32), out_a)

            @pl.when(chip > 0)
            def _():
                for start in range(0, rows, block):
                    total = base_a[pl.ds(start, block), :].astype(F32) + product(core, start, in_ref)
                    finish(core, start, total, out_a)

            for start in range(0, rows, block):
                total = base_b[pl.ds(start, block), :].astype(F32) + product(1 - core, start, out_a)
                finish(1 - core, start, total, out_b)

    shape = jax.ShapeDtypeStruct((rows, LANES), BF16)
    given = [front for chunk in chunks for front in fronts[chunk]]
    return pl.pallas_call(
        body,
        out_shape=(shape, shape),
        in_specs=[VMEM] * (5 + len(given)) + [ANY] * len(after),
        out_specs=(VMEM, VMEM),
        scratch_shapes=[pltpu.VMEM((rows, LANES), BF16)] * 2,
        compiler_params=PARAMS,
        cost_estimate=cost(2 * rows * rows * 64, rows * LANES),
        name="tick",
    )(kernels, factors, incoming, *given, *before, *after)


def star_stage(candidates, forward, backward, weights, owners):
    rows = candidates[0].shape[0]
    stages = len(candidates) // 2
    panel = rows // owners
    orbitals = backward.shape[0]
    width = HALF // owners

    def body(*refs):
        inputs = refs[: len(candidates)]
        forward_ref, backward_ref, weight_ref = refs[len(candidates) : len(candidates) + 3]
        out_refs = refs[len(candidates) + 3 : len(candidates) + 3 + owners]
        green_ref = refs[-1]
        index = lax.axis_index("tm")
        core = lax.rem(index, 2)
        chip = index // 2
        place = lax.axis_index("mom")
        for stage in range(stages):
            for parity in range(2):

                @pl.when((chip == stage) & (core == parity))
                def _():
                    for slot in range(2):
                        green_ref[slot] = inputs[2 * stage + (parity + slot) % 2][...]

        def mix(x, table_ref):
            groups = x.reshape(panel // orbitals, orbitals, LANES)
            total = groups * table_ref[0]
            for shift in range(1, orbitals):
                total += pltpu.roll(groups, shift, 1) * table_ref[shift]
            return total.reshape(panel, LANES)

        for slot in range(2):
            blocks = []
            for q in range(owners):
                rotated = mix(green_ref[slot, pl.ds(q * panel, panel), :].astype(F32), forward_ref)
                green = rotated * weight_ref[0, :1]
                for step in range(1, owners):
                    green += turn(rotated, width * step) * weight_ref[step, :1]
                square = green * green
                sigma = (square + pltpu.roll(square, HALF, 1)) * green
                blocks.append(mix(sigma, backward_ref))

            def store(step, message):
                out_refs[step][slot] = message

            to_messages(blocks, owners, place, store)

    shape = jax.ShapeDtypeStruct((2, panel, LANES), BF16)
    return pl.pallas_call(
        body,
        out_shape=(shape,) * owners,
        in_specs=[VMEM] * (len(candidates) + 3),
        out_specs=(VMEM,) * owners,
        scratch_shapes=[pltpu.VMEM((2, rows, LANES), BF16)],
        compiler_params=PARAMS,
        cost_estimate=cost(0, 16 * rows * LANES),
        name="stars",
    )(*candidates, forward, backward, weights)


def restore(kept, got):
    owners = len(kept)
    panel = kept[0].shape[1]

    def body(*refs):
        place = lax.axis_index("mom")
        for side in range(2):
            messages = [refs[d][0] if side == 0 else refs[owners][d] for d in range(owners)]
            for q, block in enumerate(from_messages(messages, owners, place)):
                refs[-1][side, pl.ds(q * panel, panel), :] = block.astype(BF16)

    return pl.pallas_call(
        body,
        out_shape=jax.ShapeDtypeStruct((2, owners * panel, LANES), BF16),
        in_specs=[VMEM] * (owners + 1),
        out_specs=VMEM,
        compiler_params=PARAMS,
        cost_estimate=cost(0, 8 * owners * panel * LANES),
        name="restore",
    )(*kept, got)


def assemble(restored, kept, got, columns):
    owners = len(kept)
    panel = kept[0].shape[1]
    count = len(restored)

    def body(*refs):
        out_ref = refs[-1]
        core = lax.rem(lax.axis_index("tm"), 2)
        place = lax.axis_index("mom")
        low = lane_index((panel, LANES)) < HALF
        for side in range(2):
            half = core if side == 0 else 1 - core
            messages = [refs[count + d][0] if side == 0 else refs[count + owners][d] for d in range(owners)]
            last = from_messages(messages, owners, place)
            for pair in range((count + 1) // 2):
                start = pl.multiple_of(half * (columns // 2) + pair * LANES, LANES)
                for q in range(owners):
                    span = pl.ds(q * panel, panel)
                    first = refs[2 * pair][side, span, :].astype(F32)
                    second = last[q] if 2 * pair + 1 == count else refs[2 * pair + 1][side, span, :].astype(F32)
                    out_ref[0, span, pl.ds(start, LANES)] = jnp.where(low, first, pltpu.roll(second, HALF, 1)).astype(BF16)
                    out_ref[1, span, pl.ds(start, LANES)] = jnp.where(low, pltpu.roll(first, HALF, 1), second).astype(BF16)

    given = [*restored, *kept, got]
    return pl.pallas_call(
        body,
        out_shape=jax.ShapeDtypeStruct((2, owners * panel, columns), BF16),
        in_specs=[VMEM] * len(given),
        out_specs=VMEM,
        compiler_params=PARAMS,
        cost_estimate=cost(0, 8 * owners * panel * columns),
        name="assemble",
    )(*given)


def star_tables(rotation, star_of):
    points, orbitals = rotation.shape[:2]
    width = HALF // points

    def body(rotation_ref, star_ref, forward_ref, backward_ref, weight_ref):
        shape = (orbitals, LANES)
        point = lane_block(shape, points)
        row = lax.broadcasted_iota(jnp.int32, shape, 0)
        columns = []
        for column in range(orbitals):
            total = jnp.zeros(shape, F32)
            for k in range(points):
                entry = rotation_ref[k].astype(F32)[:, column : column + 1]
                total = jnp.where(point == k, jnp.broadcast_to(entry, shape), total)
            columns.append(total)
        for shift in range(orbitals):
            forward = jnp.zeros(shape, F32)
            backward = jnp.zeros(shape, F32)
            for column in range(orbitals):
                here = lax.rem(row - shift + orbitals, orbitals) == column
                forward = jnp.where(here, columns[column], forward)
                moved = columns[column] if shift == 0 else pltpu.roll(columns[column], shift, 0)
                backward = jnp.where(row == column, moved, backward)
            forward_ref[shift] = forward
            backward_ref[shift] = backward
        star = jnp.zeros(shape, F32)
        for k in range(points):
            star = jnp.where(point == k, star_ref[k].astype(F32), star)
        same = [jnp.where(star == turn(star, width * step), 1.0, 0.0) for step in range(points)]
        count = functools.reduce(jnp.add, same)
        for step in range(points):
            weight_ref[step] = same[step] / count

    return pl.pallas_call(
        body,
        out_shape=(
            jax.ShapeDtypeStruct((orbitals, orbitals, LANES), F32),
            jax.ShapeDtypeStruct((orbitals, orbitals, LANES), F32),
            jax.ShapeDtypeStruct((points, orbitals, LANES), F32),
        ),
        in_specs=[VMEM, pl.BlockSpec(memory_space=pltpu.SMEM)],
        out_specs=(VMEM,) * 3,
        compiler_params=PARAMS,
        cost_estimate=cost(0, 12 * orbitals * orbitals * LANES),
        name="tables",
    )(rotation, star_of)


def shards(kernel, dinv, source, rotation, star_of):
    tiles = lax.axis_size("tm")
    owners = lax.axis_size("mom")
    rows = source.shape[2]
    columns = source.shape[4]
    stages = tiles // 2
    chunks = columns // LANES
    items = chunks * SECTIONS
    trade = functools.partial(lax.ppermute, axis_name="tm", perm=[(i, i ^ 1) for i in range(tiles)])
    onward = functools.partial(lax.ppermute, axis_name="tm", perm=[(i, i + 2) for i in range(tiles - 2)])

    def deliver(messages):
        kept = [messages[0]]
        for step in range(1, owners):
            kept.append(lax.ppermute(messages[step], "mom", [(i, (i + step) % owners) for i in range(owners)]))
        return kept

    own_kernel = kernel.reshape(2 * rows, rows)
    other_kernel = trade(own_kernel)
    planes = source.reshape(2, rows, columns)
    stay = functools.partial(pltpu.with_memory_space_constraint, memory_space=pltpu.HBM)
    *packed, kernels = pack_fronts(stay(planes), 0, owners, stay(dinv.reshape(2 * rows // LANES, LANES)), stay(own_kernel))
    tables = star_tables(rotation, star_of)
    ready = pack_fronts(planes, 1, owners, after=(packed[0], tables[0]))
    kept = deliver(packed)
    got = trade(stack_other(kept, ready[:1]))
    front_a, front_b, factors, kernels = unpack_fronts(kept, got, rows, kernels, other_kernel)
    fronts = [(front_a, front_b)]
    kept = deliver(ready)

    incoming = [front_a] * DELAY
    before = (front_a, front_b)
    solved, chunked = [], []
    for time in range(items + DELAY * (stages - 1)):
        starting = {}
        for stage in range(stages):
            item = time - DELAY * stage
            if 0 <= item < items and item % SECTIONS == 0:
                starting[item // SECTIONS] = fronts[item // SECTIONS]
        before = tick(time, kernels, factors, starting, incoming[time], before, items, [])
        solved.append(before)
        incoming.append(onward(before[1]))
        chunk = time // SECTIONS + 1
        if 1 < chunk < chunks and time % SECTIONS == 0:
            kept = deliver(pack_fronts(planes, chunk, owners, after=before[1:]))
        if chunk < chunks and time % SECTIONS == SECTIONS - 1:
            fronts.append(unpack_fronts(kept, trade(stack_other(kept, (before[1], incoming[time + 1]))), rows))
        last = time - DELAY * (stages - 1)
        if last >= 0 and last % SECTIONS == SECTIONS - 1:
            candidates = []
            for stage in range(stages):
                candidates.extend(solved[last + DELAY * stage])
            chunked.append(deliver(star_stage(candidates, *tables, owners)))
    restored = []
    for back in chunked[:-1]:
        restored.append(restore(back, trade(stack_other(back, chunked[-1][1:9]))))
    back = chunked[-1]
    return assemble(restored, back, trade(stack_other(back, restored)), columns).reshape(1, 2, rows, 1, columns)


def solution(mesh):
    in_specs = (
        P("tm", None, None, None),
        P("tm", None, None, "mom"),
        P("tm", None, None, "mom", None),
        P(),
        P(),
    )
    out_specs = P("tm", None, None, "mom", None)
    return jax.shard_map(shards, mesh=mesh, in_specs=in_specs, out_specs=out_specs, check_vma=False)
```

```python
import functools

import jax
import jax.numpy as jnp
from jax import lax
from jax.experimental import pallas as pl
from jax.experimental.pallas import tpu as pltpu
from jax.sharding import PartitionSpec as P

SECTIONS = 3
LANES = 128
HALF = LANES // 2
DELAY = 2
BLOCK = 256

VMEM = pl.BlockSpec(memory_space=pltpu.VMEM)
ANY = pl.BlockSpec(memory_space=pl.ANY)
F32 = jnp.float32
BF16 = jnp.bfloat16


PARAMS = pltpu.CompilerParams(vmem_limit_bytes=16 * 2**20)


def cost(flops, moved):
    return pl.CostEstimate(flops=flops, bytes_accessed=moved, transcendentals=0)


def lane_index(shape):
    return lax.broadcasted_iota(jnp.int32, shape, len(shape) - 1)


def turn(x, shift, half=HALF):
    shift %= half
    if shift == 0:
        return x
    inside = (lane_index(x.shape) & (half - 1)) >= shift
    return jnp.where(inside, pltpu.roll(x, shift, 1), pltpu.roll(x, shift + half, 1))


def lane_block(shape, owners):
    return (lane_index(shape) & (HALF - 1)) >> ((HALF // owners).bit_length() - 1)


def wrap(x, owners):
    return (x + 2 * owners) & (owners - 1)


def to_messages(blocks, owners, place, store):
    width = HALF // owners
    turned = [turn(block, width * q) for q, block in enumerate(blocks)]
    lanes = lane_block(blocks[0].shape, owners)
    for step in range(owners):
        panel = wrap(lanes - place - step, owners)
        message = turned[0]
        for q in range(1, owners):
            message = jnp.where(panel == q, turned[q], message)
        store(step, message.astype(BF16))


def from_messages(messages, owners, place):
    width = HALF // owners
    turned = [turn(message.astype(F32), width * ((owners - step) % owners)) for step, message in enumerate(messages)]
    lanes = lane_block(messages[0].shape, owners)
    panels = []
    for q in range(owners):
        step_of = wrap(place - lanes + q, owners)
        panel = turned[0]
        for step in range(1, owners):
            panel = jnp.where(step_of == step, turned[step], panel)
        panels.append(turn(panel, HALF - width * q))
    return panels


def pack_fronts(source, chunk, owners, dinv=None, after=()):
    rows, columns = source.shape[1:]
    panel = rows // owners
    leading = dinv is not None
    extra = 3 * dinv.shape[0] if leading else 0

    def body(source_ref, *refs):
        core = lax.rem(lax.axis_index("tm"), 2)
        place = lax.axis_index("mom")
        low = lane_index((panel, LANES)) < HALF
        out_refs = refs[1:] if leading else refs[len(after) :]
        if leading:
            dinv_hbm, plane_hbm = refs[0], source_ref
            source_ref, dinv_ref, sems = refs[1 + owners :]
            loads = [
                pltpu.make_async_copy(dinv_hbm, dinv_ref, sems.at[0]),
                pltpu.make_async_copy(plane_hbm, source_ref, sems.at[1]),
            ]
            for load in loads:
                load.start()
            loads[0].wait()
            loads[1].wait()
            first = dinv_ref[...].astype(BF16)
            rest = dinv_ref[...] - first.astype(F32)
            second = rest.astype(BF16)
            third = (rest - second.astype(F32)).astype(BF16)
            pieces = jnp.concatenate([first, second, third])
        for slot in range(2):
            half = core if slot == 0 else 1 - core
            start = pl.multiple_of(half * (columns // 2) + chunk // 2 * LANES, LANES)
            blocks = []
            for q in range(owners):
                real = source_ref[0, pl.ds(q * panel, panel), pl.ds(start, LANES)].astype(F32)
                imag = source_ref[1, pl.ds(q * panel, panel), pl.ds(start, LANES)].astype(F32)
                if chunk % 2 == 0:
                    blocks.append(jnp.where(low, real, pltpu.roll(imag, HALF, 1)))
                else:
                    blocks.append(jnp.where(low, pltpu.roll(real, HALF, 1), imag))

            def store(step, message):
                out_refs[step][slot, pl.ds(0, panel), :] = message

            to_messages(blocks, owners, place, store)
            if leading:
                for step in range(owners):
                    out_refs[step][slot, pl.ds(panel, extra), :] = pieces

    shapes = [jax.ShapeDtypeStruct((2, panel + extra, LANES), BF16)] * owners
    scratch = []
    if leading:
        scratch = [pltpu.VMEM(source.shape, BF16), pltpu.VMEM(dinv.shape, F32), pltpu.SemaphoreType.DMA((2,))]
    given = (dinv,) if leading else tuple(after)
    return pl.pallas_call(
        body,
        out_shape=tuple(shapes),
        in_specs=[ANY] * 2 if leading else [VMEM] + [ANY] * len(after),
        out_specs=(VMEM,) * len(shapes),
        scratch_shapes=scratch,
        compiler_params=PARAMS,
        cost_estimate=cost(0, 2 * rows * columns * 2),
        name="pack",
    )(source, *given)


def stack_other(kept, after):
    owners = len(kept)

    def body(*refs):
        for step in range(owners):
            refs[-1][step] = refs[step][1]

    return pl.pallas_call(
        body,
        out_shape=jax.ShapeDtypeStruct((owners,) + kept[0].shape[1:], BF16),
        in_specs=[VMEM] * owners + [ANY] * len(after),
        out_specs=VMEM,
        compiler_params=PARAMS,
        cost_estimate=cost(0, 2 * kept[0].size * owners),
        name="stack",
    )(*kept, *after)


def unpack_fronts(kept, got, rows, kernels=None, other_kernel=None):
    owners = len(kept)
    panel = rows // owners
    blocks = rows // LANES
    extra = kept[0].shape[1] - panel
    leading = kernels is not None

    def body(*refs):
        kept_refs, got_ref = refs[:owners], refs[owners]
        place = lax.axis_index("mom")
        if leading:
            other_ref, outs, hold_ref, sem = refs[owners + 2], refs[owners + 3 : owners + 6], refs[owners + 6], refs[owners + 7]
            load = pltpu.make_async_copy(other_ref, hold_ref.at[1], sem)
            load.start()
        else:
            outs = refs[owners + 1 :]
        for tile in range(2):
            read = (lambda step, span: kept_refs[step][0, span, :]) if tile == 0 else (lambda step, span: got_ref[step, span, :])
            panels = from_messages([read(step, pl.ds(0, panel)) for step in range(owners)], owners, place)
            for q in range(owners):
                outs[tile][pl.ds(q * panel, panel), :] = panels[q].astype(BF16)
            if not leading:
                continue
            pieces = jnp.concatenate([read(step, pl.ds(panel, extra)) for step in range(owners)])
            shape = (owners * extra, LANES)
            row = lax.broadcasted_iota(jnp.int32, shape, 0)
            owner = wrap(place - row // extra, owners)
            wanted = owner == lane_block(shape, owners)
            inner = lax.rem(lax.rem(row, extra), 2 * blocks)
            sign = jnp.where(lane_index(shape) < HALF, -1.0, 1.0)
            for part in range(2):
                scale = jnp.ones(shape, F32) if part == 0 else sign
                for block in range(blocks):
                    pick = jnp.where(wanted & (inner == part * blocks + block), scale, 0.0).astype(BF16)
                    spread = lax.dot_general(pieces, pick, (((0,), (0,)), ((), ())), preferred_element_type=F32)
                    outs[2][tile, part, pl.ds(block * LANES, LANES), :] = spread
        if leading:
            load.wait()

    shapes = [jax.ShapeDtypeStruct((rows, LANES), BF16)] * 2
    given = [*kept, got]
    aliases = {}
    if leading:
        shapes += [pltpu.VMEM((2, 2, rows, LANES), F32), pltpu.VMEM(kernels.shape, kernels.dtype)]
        aliases = {len(given): 3}
        given += [kernels, other_kernel]
    return pl.pallas_call(
        body,
        out_shape=tuple(shapes),
        in_specs=[VMEM] * (owners + 1) + ([VMEM, ANY] if leading else []),
        out_specs=(VMEM,) * len(shapes),
        scratch_shapes=[pltpu.SemaphoreType.DMA] if leading else [],
        input_output_aliases=aliases,
        compiler_params=PARAMS,
        cost_estimate=cost(0, 8 * rows * LANES),
        name="unpack_first" if leading else "unpack_next",
    )(*given)


def tick(time, kernels, factors, fronts, incoming, before, items, after):
    rows = incoming.shape[0]
    block = min(rows, BLOCK)
    chunks = sorted(fronts)

    def body(kernel_ref, factor_ref, in_ref, *refs):
        front_refs = refs[: 2 * len(chunks)]
        before_a, before_b, out_a, out_b, base_a, base_b = refs[2 * len(chunks) :][:2] + refs[-4:]
        index = lax.axis_index("tm")
        core = lax.rem(index, 2)
        chip = index // 2
        item = time - DELAY * chip
        section = lax.rem(item + SECTIONS * 64, SECTIONS)
        sign = jnp.where(lane_index((block, LANES)) < HALF, -1.0, 1.0).astype(F32)

        def finish(slot, start, total, target):
            span = pl.ds(start, block)
            turned = pltpu.roll(total, HALF, 1)
            target[span, :] = (factor_ref[slot, 0, span, :] * total + factor_ref[slot, 1, span, :] * turned).astype(BF16)

        def product(slot, start, x_ref):
            real = jnp.dot(kernel_ref[slot, pl.ds(start, block), :], x_ref[...], preferred_element_type=F32)
            imag = jnp.dot(kernel_ref[slot, pl.ds(rows + start, block), :], x_ref[...], preferred_element_type=F32)
            return real + pltpu.roll(imag, HALF, 1) * sign

        @pl.when((item >= 0) & (item < items))
        def _():
            for place, chunk in enumerate(chunks):
                for parity in range(2):

                    @pl.when((item == chunk * SECTIONS) & (core == parity))
                    def _():
                        base_a[...] = front_refs[2 * place + parity][...]
                        base_b[...] = front_refs[2 * place + 1 - parity][...]

            @pl.when(section > 0)
            def _():
                base_a[...] = before_a[...]
                base_b[...] = before_b[...]

            @pl.when(chip == 0)
            def _():
                for start in range(0, rows, block):
                    finish(core, start, base_a[pl.ds(start, block), :].astype(F32), out_a)

            @pl.when(chip > 0)
            def _():
                for start in range(0, rows, block):
                    total = base_a[pl.ds(start, block), :].astype(F32) + product(core, start, in_ref)
                    finish(core, start, total, out_a)

            for start in range(0, rows, block):
                total = base_b[pl.ds(start, block), :].astype(F32) + product(1 - core, start, out_a)
                finish(1 - core, start, total, out_b)

    shape = jax.ShapeDtypeStruct((rows, LANES), BF16)
    given = [front for chunk in chunks for front in fronts[chunk]]
    return pl.pallas_call(
        body,
        out_shape=(shape, shape),
        in_specs=[VMEM] * (5 + len(given)) + [ANY] * len(after),
        out_specs=(VMEM, VMEM),
        scratch_shapes=[pltpu.VMEM((rows, LANES), BF16)] * 2,
        compiler_params=PARAMS,
        cost_estimate=cost(2 * rows * rows * 64, rows * LANES),
        name="tick",
    )(kernels, factors, incoming, *given, *before, *after)


def star_stage(candidates, forward, backward, weights, owners):
    rows = candidates[0].shape[0]
    stages = len(candidates) // 2
    panel = rows // owners
    orbitals = backward.shape[0]
    width = HALF // owners

    def body(*refs):
        inputs = refs[: len(candidates)]
        forward_ref, backward_ref, weight_ref = refs[len(candidates) : len(candidates) + 3]
        out_refs = refs[len(candidates) + 3 : len(candidates) + 3 + owners]
        green_ref = refs[-1]
        index = lax.axis_index("tm")
        core = lax.rem(index, 2)
        chip = index // 2
        place = lax.axis_index("mom")
        for stage in range(stages):
            for parity in range(2):

                @pl.when((chip == stage) & (core == parity))
                def _():
                    for slot in range(2):
                        green_ref[slot] = inputs[2 * stage + (parity + slot) % 2][...]

        def mix(x, table_ref):
            groups = x.reshape(panel // orbitals, orbitals, LANES)
            total = groups * table_ref[0]
            for shift in range(1, orbitals):
                total += pltpu.roll(groups, shift, 1) * table_ref[shift]
            return total.reshape(panel, LANES)

        for slot in range(2):
            blocks = []
            for q in range(owners):
                rotated = mix(green_ref[slot, pl.ds(q * panel, panel), :].astype(F32), forward_ref)
                green = rotated * weight_ref[0, :1]
                for step in range(1, owners):
                    green += turn(rotated, width * step) * weight_ref[step, :1]
                square = green * green
                sigma = (square + pltpu.roll(square, HALF, 1)) * green
                blocks.append(mix(sigma, backward_ref))

            def store(step, message):
                out_refs[step][slot] = message

            to_messages(blocks, owners, place, store)

    shape = jax.ShapeDtypeStruct((2, panel, LANES), BF16)
    return pl.pallas_call(
        body,
        out_shape=(shape,) * owners,
        in_specs=[VMEM] * (len(candidates) + 3),
        out_specs=(VMEM,) * owners,
        scratch_shapes=[pltpu.VMEM((2, rows, LANES), BF16)],
        compiler_params=PARAMS,
        cost_estimate=cost(0, 16 * rows * LANES),
        name="stars",
    )(*candidates, forward, backward, weights)


def restore(kept, got):
    owners = len(kept)
    panel = kept[0].shape[1]

    def body(*refs):
        place = lax.axis_index("mom")
        for side in range(2):
            messages = [refs[d][0] if side == 0 else refs[owners][d] for d in range(owners)]
            for q, block in enumerate(from_messages(messages, owners, place)):
                refs[-1][side, pl.ds(q * panel, panel), :] = block.astype(BF16)

    return pl.pallas_call(
        body,
        out_shape=jax.ShapeDtypeStruct((2, owners * panel, LANES), BF16),
        in_specs=[VMEM] * (owners + 1),
        out_specs=VMEM,
        compiler_params=PARAMS,
        cost_estimate=cost(0, 8 * owners * panel * LANES),
        name="restore",
    )(*kept, got)


def assemble(restored, kept, got, columns):
    owners = len(kept)
    panel = kept[0].shape[1]
    count = len(restored)

    def body(*refs):
        out_ref = refs[-1]
        core = lax.rem(lax.axis_index("tm"), 2)
        place = lax.axis_index("mom")
        low = lane_index((panel, LANES)) < HALF
        for side in range(2):
            half = core if side == 0 else 1 - core
            messages = [refs[count + d][0] if side == 0 else refs[count + owners][d] for d in range(owners)]
            last = from_messages(messages, owners, place)
            for pair in range((count + 1) // 2):
                start = pl.multiple_of(half * (columns // 2) + pair * LANES, LANES)
                for q in range(owners):
                    span = pl.ds(q * panel, panel)
                    first = refs[2 * pair][side, span, :].astype(F32)
                    second = last[q] if 2 * pair + 1 == count else refs[2 * pair + 1][side, span, :].astype(F32)
                    out_ref[0, span, pl.ds(start, LANES)] = jnp.where(low, first, pltpu.roll(second, HALF, 1)).astype(BF16)
                    out_ref[1, span, pl.ds(start, LANES)] = jnp.where(low, pltpu.roll(first, HALF, 1), second).astype(BF16)

    given = [*restored, *kept, got]
    return pl.pallas_call(
        body,
        out_shape=jax.ShapeDtypeStruct((2, owners * panel, columns), BF16),
        in_specs=[VMEM] * len(given),
        out_specs=VMEM,
        compiler_params=PARAMS,
        cost_estimate=cost(0, 8 * owners * panel * columns),
        name="assemble",
    )(*given)


def star_tables(rotation, star_of, own_kernel):
    points, orbitals = rotation.shape[:2]
    width = HALF // points

    def body(rotation_ref, star_ref, own_ref, forward_ref, backward_ref, weight_ref, hold_ref, sem):
        load = pltpu.make_async_copy(own_ref, hold_ref.at[0], sem)
        load.start()
        shape = (orbitals, LANES)
        point = lane_block(shape, points)
        row = lax.broadcasted_iota(jnp.int32, shape, 0)
        columns = []
        for column in range(orbitals):
            total = jnp.zeros(shape, F32)
            for k in range(points):
                entry = rotation_ref[k].astype(F32)[:, column : column + 1]
                total = jnp.where(point == k, jnp.broadcast_to(entry, shape), total)
            columns.append(total)
        for shift in range(orbitals):
            forward = jnp.zeros(shape, F32)
            backward = jnp.zeros(shape, F32)
            for column in range(orbitals):
                here = lax.rem(row - shift + orbitals, orbitals) == column
                forward = jnp.where(here, columns[column], forward)
                moved = columns[column] if shift == 0 else pltpu.roll(columns[column], shift, 0)
                backward = jnp.where(row == column, moved, backward)
            forward_ref[shift] = forward
            backward_ref[shift] = backward
        star = jnp.zeros(shape, F32)
        for k in range(points):
            star = jnp.where(point == k, star_ref[k].astype(F32), star)
        same = [jnp.where(star == turn(star, width * step), 1.0, 0.0) for step in range(points)]
        count = functools.reduce(jnp.add, same)
        for step in range(points):
            weight_ref[step] = same[step] / count
        load.wait()

    return pl.pallas_call(
        body,
        out_shape=(
            jax.ShapeDtypeStruct((orbitals, orbitals, LANES), F32),
            jax.ShapeDtypeStruct((orbitals, orbitals, LANES), F32),
            jax.ShapeDtypeStruct((points, orbitals, LANES), F32),
            pltpu.VMEM((2,) + own_kernel.shape, own_kernel.dtype),
        ),
        in_specs=[VMEM, pl.BlockSpec(memory_space=pltpu.SMEM), ANY],
        out_specs=(VMEM,) * 4,
        scratch_shapes=[pltpu.SemaphoreType.DMA],
        compiler_params=PARAMS,
        cost_estimate=cost(0, 12 * orbitals * orbitals * LANES),
        name="tables",
    )(rotation, star_of, own_kernel)


def shards(kernel, dinv, source, rotation, star_of):
    tiles = lax.axis_size("tm")
    owners = lax.axis_size("mom")
    rows = source.shape[2]
    columns = source.shape[4]
    stages = tiles // 2
    chunks = columns // LANES
    items = chunks * SECTIONS
    trade = functools.partial(lax.ppermute, axis_name="tm", perm=[(i, i ^ 1) for i in range(tiles)])
    onward = functools.partial(lax.ppermute, axis_name="tm", perm=[(i, i + 2) for i in range(tiles - 2)])

    def deliver(messages):
        kept = [messages[0]]
        for step in range(1, owners):
            kept.append(lax.ppermute(messages[step], "mom", [(i, (i + step) % owners) for i in range(owners)]))
        return kept

    own_kernel = kernel.reshape(2 * rows, rows)
    other_kernel = trade(own_kernel)
    planes = source.reshape(2, rows, columns)
    stay = functools.partial(pltpu.with_memory_space_constraint, memory_space=pltpu.HBM)
    packed = pack_fronts(stay(planes), 0, owners, stay(dinv.reshape(2 * rows // LANES, LANES)))
    *tables, kernels = star_tables(rotation, star_of, stay(own_kernel))
    ready = pack_fronts(planes, 1, owners, after=(packed[0], tables[0]))
    kept = deliver(packed)
    got = trade(stack_other(kept, ready[:1]))
    front_a, front_b, factors, kernels = unpack_fronts(kept, got, rows, kernels, other_kernel)
    fronts = [(front_a, front_b)]
    kept = deliver(ready)

    incoming = [front_a] * DELAY
    before = (front_a, front_b)
    solved, chunked = [], []
    for time in range(items + DELAY * (stages - 1)):
        starting = {}
        for stage in range(stages):
            item = time - DELAY * stage
            if 0 <= item < items and item % SECTIONS == 0:
                starting[item // SECTIONS] = fronts[item // SECTIONS]
        before = tick(time, kernels, factors, starting, incoming[time], before, items, [])
        solved.append(before)
        incoming.append(onward(before[1]))
        chunk = time // SECTIONS + 1
        if 1 < chunk < chunks and time % SECTIONS == 0:
            kept = deliver(pack_fronts(planes, chunk, owners, after=before[1:]))
        if chunk < chunks and time % SECTIONS == SECTIONS - 1:
            fronts.append(unpack_fronts(kept, trade(stack_other(kept, (before[1], incoming[time + 1]))), rows))
        last = time - DELAY * (stages - 1)
        if last >= 0 and last % SECTIONS == SECTIONS - 1:
            candidates = []
            for stage in range(stages):
                candidates.extend(solved[last + DELAY * stage])
            chunked.append(deliver(star_stage(candidates, *tables, owners)))
    restored = []
    for back in chunked[:-1]:
        restored.append(restore(back, trade(stack_other(back, chunked[-1][1:9]))))
    back = chunked[-1]
    return assemble(restored, back, trade(stack_other(back, ())), columns).reshape(1, 2, rows, 1, columns)


def solution(mesh):
    in_specs = (
        P("tm", None, None, None),
        P("tm", None, None, "mom"),
        P("tm", None, None, "mom", None),
        P(),
        P(),
    )
    out_specs = P("tm", None, None, "mom", None)
    return jax.shard_map(shards, mesh=mesh, in_specs=in_specs, out_specs=out_specs, check_vma=False)
```

```python
import functools

import jax
import jax.numpy as jnp
from jax import lax
from jax.experimental import pallas as pl
from jax.experimental.pallas import tpu as pltpu
from jax.sharding import PartitionSpec as P

SECTIONS = 3
LANES = 128
HALF = LANES // 2
DELAY = 2
BLOCK = 256

VMEM = pl.BlockSpec(memory_space=pltpu.VMEM)
ANY = pl.BlockSpec(memory_space=pl.ANY)
F32 = jnp.float32
BF16 = jnp.bfloat16


PARAMS = pltpu.CompilerParams(vmem_limit_bytes=16 * 2**20)


def cost(flops, moved):
    return pl.CostEstimate(flops=flops, bytes_accessed=moved, transcendentals=0)


def lane_index(shape):
    return lax.broadcasted_iota(jnp.int32, shape, len(shape) - 1)


def turn(x, shift, half=HALF):
    shift %= half
    if shift == 0:
        return x
    inside = (lane_index(x.shape) & (half - 1)) >= shift
    return jnp.where(inside, pltpu.roll(x, shift, 1), pltpu.roll(x, shift + half, 1))


def lane_block(shape, owners):
    return (lane_index(shape) & (HALF - 1)) >> ((HALF // owners).bit_length() - 1)


def wrap(x, owners):
    return (x + 2 * owners) & (owners - 1)


def to_messages(blocks, owners, place, store):
    width = HALF // owners
    turned = [turn(block, width * q) for q, block in enumerate(blocks)]
    lanes = lane_block(blocks[0].shape, owners)
    for step in range(owners):
        panel = wrap(lanes - place - step, owners)
        message = turned[0]
        for q in range(1, owners):
            message = jnp.where(panel == q, turned[q], message)
        store(step, message.astype(BF16))


def from_messages(messages, owners, place):
    width = HALF // owners
    turned = [turn(message.astype(F32), width * ((owners - step) % owners)) for step, message in enumerate(messages)]
    lanes = lane_block(messages[0].shape, owners)
    panels = []
    for q in range(owners):
        step_of = wrap(place - lanes + q, owners)
        panel = turned[0]
        for step in range(1, owners):
            panel = jnp.where(step_of == step, turned[step], panel)
        panels.append(turn(panel, HALF - width * q))
    return panels


def pack_fronts(source, chunk, owners, dinv=None, after=()):
    rows, columns = source.shape[1:]
    panel = rows // owners
    leading = dinv is not None
    extra = 3 * dinv.shape[0] if leading else 0

    def body(source_ref, *refs):
        core = lax.rem(lax.axis_index("tm"), 2)
        place = lax.axis_index("mom")
        low = lane_index((panel, LANES)) < HALF
        out_refs = refs[1:] if leading else refs[len(after) :]
        if leading:
            dinv_hbm, plane_hbm = refs[0], source_ref
            source_ref, dinv_ref, sems = refs[1 + owners :]
            loads = [
                pltpu.make_async_copy(dinv_hbm, dinv_ref, sems.at[0]),
                pltpu.make_async_copy(plane_hbm, source_ref, sems.at[1]),
            ]
            for load in loads:
                load.start()
            loads[0].wait()
            loads[1].wait()
            first = dinv_ref[...].astype(BF16)
            rest = dinv_ref[...] - first.astype(F32)
            second = rest.astype(BF16)
            third = (rest - second.astype(F32)).astype(BF16)
            pieces = jnp.concatenate([first, second, third])
        for slot in range(2):
            half = core if slot == 0 else 1 - core
            start = pl.multiple_of(half * (columns // 2) + chunk // 2 * LANES, LANES)
            blocks = []
            for q in range(owners):
                real = source_ref[0, pl.ds(q * panel, panel), pl.ds(start, LANES)].astype(F32)
                imag = source_ref[1, pl.ds(q * panel, panel), pl.ds(start, LANES)].astype(F32)
                if chunk % 2 == 0:
                    blocks.append(jnp.where(low, real, pltpu.roll(imag, HALF, 1)))
                else:
                    blocks.append(jnp.where(low, pltpu.roll(real, HALF, 1), imag))

            def store(step, message):
                out_refs[step][pl.ds(slot * panel, panel), :] = message

            to_messages(blocks, owners, place, store)
        if leading:
            for step in range(owners):
                out_refs[step][pl.ds(2 * panel, extra), :] = pieces

    shapes = [jax.ShapeDtypeStruct((2 * panel + extra, LANES), BF16)] * owners
    scratch = []
    if leading:
        scratch = [pltpu.VMEM(source.shape, BF16), pltpu.VMEM(dinv.shape, F32), pltpu.SemaphoreType.DMA((2,))]
    given = (dinv,) if leading else tuple(after)
    return pl.pallas_call(
        body,
        out_shape=tuple(shapes),
        in_specs=[ANY] * 2 if leading else [VMEM] + [ANY] * len(after),
        out_specs=(VMEM,) * len(shapes),
        scratch_shapes=scratch,
        compiler_params=PARAMS,
        cost_estimate=cost(0, 2 * rows * columns * 2),
        name="pack",
    )(source, *given)


def stack_other(kept, panel, after):
    owners = len(kept)
    rest = kept[0].shape[0] - panel

    def body(*refs):
        for step in range(owners):
            refs[-1][step] = refs[step][pl.ds(panel, rest), :]

    return pl.pallas_call(
        body,
        out_shape=jax.ShapeDtypeStruct((owners, rest, LANES), BF16),
        in_specs=[VMEM] * owners + [ANY] * len(after),
        out_specs=VMEM,
        compiler_params=PARAMS,
        cost_estimate=cost(0, 4 * owners * rest * LANES),
        name="stack",
    )(*kept, *after)


def unpack_fronts(kept, got, rows, kernels=None, other_kernel=None):
    owners = len(kept)
    panel = rows // owners
    blocks = rows // LANES
    extra = kept[0].shape[0] - 2 * panel
    leading = kernels is not None

    def body(*refs):
        kept_refs, got_ref = refs[:owners], refs[owners]
        place = lax.axis_index("mom")
        if leading:
            other_ref, outs, hold_ref, sem = refs[owners + 2], refs[owners + 3 : owners + 6], refs[owners + 6], refs[owners + 7]
            load = pltpu.make_async_copy(other_ref, hold_ref.at[1], sem)
            load.start()
        else:
            outs = refs[owners + 1 :]
        for tile in range(2):
            first = slice(0, panel)
            messages = [kept_refs[step][first, :] if tile == 0 else got_ref[step, first, :] for step in range(owners)]
            panels = from_messages(messages, owners, place)
            for q in range(owners):
                outs[tile][pl.ds(q * panel, panel), :] = panels[q].astype(BF16)
            if not leading:
                continue
            last = slice(2 * panel, 2 * panel + extra) if tile == 0 else slice(panel, panel + extra)
            pieces = jnp.concatenate([kept_refs[step][last, :] if tile == 0 else got_ref[step, last, :] for step in range(owners)])
            shape = (owners * extra, LANES)
            row = lax.broadcasted_iota(jnp.int32, shape, 0)
            owner = wrap(place - row // extra, owners)
            wanted = owner == lane_block(shape, owners)
            inner = lax.rem(lax.rem(row, extra), 2 * blocks)
            sign = jnp.where(lane_index(shape) < HALF, -1.0, 1.0)
            for part in range(2):
                scale = jnp.ones(shape, F32) if part == 0 else sign
                for block in range(blocks):
                    pick = jnp.where(wanted & (inner == part * blocks + block), scale, 0.0).astype(BF16)
                    spread = lax.dot_general(pieces, pick, (((0,), (0,)), ((), ())), preferred_element_type=F32)
                    outs[2][tile, part, pl.ds(block * LANES, LANES), :] = spread
        if leading:
            load.wait()

    shapes = [jax.ShapeDtypeStruct((rows, LANES), BF16)] * 2
    given = [*kept, got]
    aliases = {}
    if leading:
        shapes += [pltpu.VMEM((2, 2, rows, LANES), F32), pltpu.VMEM(kernels.shape, kernels.dtype)]
        aliases = {len(given): 3}
        given += [kernels, other_kernel]
    return pl.pallas_call(
        body,
        out_shape=tuple(shapes),
        in_specs=[VMEM] * (owners + 1) + ([VMEM, ANY] if leading else []),
        out_specs=(VMEM,) * len(shapes),
        scratch_shapes=[pltpu.SemaphoreType.DMA] if leading else [],
        input_output_aliases=aliases,
        compiler_params=PARAMS,
        cost_estimate=cost(0, 8 * rows * LANES),
        name="unpack_first" if leading else "unpack_next",
    )(*given)


def tick(time, kernels, factors, fronts, incoming, before, items, after):
    rows = incoming.shape[0]
    block = min(rows, BLOCK)
    chunks = sorted(fronts)

    def body(kernel_ref, factor_ref, in_ref, *refs):
        front_refs = refs[: 2 * len(chunks)]
        before_a, before_b, out_a, out_b, base_a, base_b = refs[2 * len(chunks) :][:2] + refs[-4:]
        index = lax.axis_index("tm")
        core = lax.rem(index, 2)
        chip = index // 2
        item = time - DELAY * chip
        section = lax.rem(item + SECTIONS * 64, SECTIONS)
        sign = jnp.where(lane_index((block, LANES)) < HALF, -1.0, 1.0).astype(F32)

        def finish(slot, start, total, target):
            span = pl.ds(start, block)
            turned = pltpu.roll(total, HALF, 1)
            target[span, :] = (factor_ref[slot, 0, span, :] * total + factor_ref[slot, 1, span, :] * turned).astype(BF16)

        def product(slot, start, x_ref):
            real = jnp.dot(kernel_ref[slot, pl.ds(start, block), :], x_ref[...], preferred_element_type=F32)
            imag = jnp.dot(kernel_ref[slot, pl.ds(rows + start, block), :], x_ref[...], preferred_element_type=F32)
            return real + pltpu.roll(imag, HALF, 1) * sign

        @pl.when((item >= 0) & (item < items))
        def _():
            for place, chunk in enumerate(chunks):
                for parity in range(2):

                    @pl.when((item == chunk * SECTIONS) & (core == parity))
                    def _():
                        base_a[...] = front_refs[2 * place + parity][...]
                        base_b[...] = front_refs[2 * place + 1 - parity][...]

            @pl.when(section > 0)
            def _():
                base_a[...] = before_a[...]
                base_b[...] = before_b[...]

            @pl.when(chip == 0)
            def _():
                for start in range(0, rows, block):
                    finish(core, start, base_a[pl.ds(start, block), :].astype(F32), out_a)

            @pl.when(chip > 0)
            def _():
                for start in range(0, rows, block):
                    total = base_a[pl.ds(start, block), :].astype(F32) + product(core, start, in_ref)
                    finish(core, start, total, out_a)

            for start in range(0, rows, block):
                total = base_b[pl.ds(start, block), :].astype(F32) + product(1 - core, start, out_a)
                finish(1 - core, start, total, out_b)

    shape = jax.ShapeDtypeStruct((rows, LANES), BF16)
    given = [front for chunk in chunks for front in fronts[chunk]]
    return pl.pallas_call(
        body,
        out_shape=(shape, shape),
        in_specs=[VMEM] * (5 + len(given)) + [ANY] * len(after),
        out_specs=(VMEM, VMEM),
        scratch_shapes=[pltpu.VMEM((rows, LANES), BF16)] * 2,
        compiler_params=PARAMS,
        cost_estimate=cost(2 * rows * rows * 64, rows * LANES),
        name="tick",
    )(kernels, factors, incoming, *given, *before, *after)


def star_stage(candidates, forward, backward, weights, owners):
    rows = candidates[0].shape[0]
    stages = len(candidates) // 2
    panel = rows // owners
    orbitals = backward.shape[0]
    width = HALF // owners

    def body(*refs):
        inputs = refs[: len(candidates)]
        forward_ref, backward_ref, weight_ref = refs[len(candidates) : len(candidates) + 3]
        out_refs = refs[len(candidates) + 3 : len(candidates) + 3 + owners]
        green_ref = refs[-1]
        index = lax.axis_index("tm")
        core = lax.rem(index, 2)
        chip = index // 2
        place = lax.axis_index("mom")
        for stage in range(stages):
            for parity in range(2):

                @pl.when((chip == stage) & (core == parity))
                def _():
                    for slot in range(2):
                        green_ref[slot] = inputs[2 * stage + (parity + slot) % 2][...]

        def mix(x, table_ref):
            groups = x.reshape(panel // orbitals, orbitals, LANES)
            total = groups * table_ref[0]
            for shift in range(1, orbitals):
                total += pltpu.roll(groups, shift, 1) * table_ref[shift]
            return total.reshape(panel, LANES)

        for slot in range(2):
            blocks = []
            for q in range(owners):
                rotated = mix(green_ref[slot, pl.ds(q * panel, panel), :].astype(F32), forward_ref)
                green = rotated * weight_ref[0, :1]
                for step in range(1, owners):
                    green += turn(rotated, width * step) * weight_ref[step, :1]
                square = green * green
                sigma = (square + pltpu.roll(square, HALF, 1)) * green
                blocks.append(mix(sigma, backward_ref))

            def store(step, message):
                out_refs[step][pl.ds(slot * panel, panel), :] = message

            to_messages(blocks, owners, place, store)

    shape = jax.ShapeDtypeStruct((2 * panel, LANES), BF16)
    return pl.pallas_call(
        body,
        out_shape=(shape,) * owners,
        in_specs=[VMEM] * (len(candidates) + 3),
        out_specs=(VMEM,) * owners,
        scratch_shapes=[pltpu.VMEM((2, rows, LANES), BF16)],
        compiler_params=PARAMS,
        cost_estimate=cost(0, 16 * rows * LANES),
        name="stars",
    )(*candidates, forward, backward, weights)


def restore(kept, got):
    owners = len(kept)
    panel = kept[0].shape[0] // 2

    def body(*refs):
        place = lax.axis_index("mom")
        for side in range(2):
            messages = [refs[d][pl.ds(0, panel), :] if side == 0 else refs[owners][d] for d in range(owners)]
            for q, block in enumerate(from_messages(messages, owners, place)):
                refs[-1][side, pl.ds(q * panel, panel), :] = block.astype(BF16)

    return pl.pallas_call(
        body,
        out_shape=jax.ShapeDtypeStruct((2, owners * panel, LANES), BF16),
        in_specs=[VMEM] * (owners + 1),
        out_specs=VMEM,
        compiler_params=PARAMS,
        cost_estimate=cost(0, 8 * owners * panel * LANES),
        name="restore",
    )(*kept, got)


def assemble(restored, kept, got, columns):
    owners = len(kept)
    panel = kept[0].shape[0] // 2
    count = len(restored)

    def body(*refs):
        out_ref = refs[-1]
        core = lax.rem(lax.axis_index("tm"), 2)
        place = lax.axis_index("mom")
        low = lane_index((panel, LANES)) < HALF
        for side in range(2):
            half = core if side == 0 else 1 - core
            messages = [refs[count + d][pl.ds(0, panel), :] if side == 0 else refs[count + owners][d] for d in range(owners)]
            last = from_messages(messages, owners, place)
            for pair in range((count + 1) // 2):
                start = pl.multiple_of(half * (columns // 2) + pair * LANES, LANES)
                for q in range(owners):
                    span = pl.ds(q * panel, panel)
                    first = refs[2 * pair][side, span, :].astype(F32)
                    second = last[q] if 2 * pair + 1 == count else refs[2 * pair + 1][side, span, :].astype(F32)
                    out_ref[0, span, pl.ds(start, LANES)] = jnp.where(low, first, pltpu.roll(second, HALF, 1)).astype(BF16)
                    out_ref[1, span, pl.ds(start, LANES)] = jnp.where(low, pltpu.roll(first, HALF, 1), second).astype(BF16)

    given = [*restored, *kept, got]
    return pl.pallas_call(
        body,
        out_shape=jax.ShapeDtypeStruct((2, owners * panel, columns), BF16),
        in_specs=[VMEM] * len(given),
        out_specs=VMEM,
        compiler_params=PARAMS,
        cost_estimate=cost(0, 8 * owners * panel * columns),
        name="assemble",
    )(*given)


def star_tables(rotation, star_of, own_kernel):
    points, orbitals = rotation.shape[:2]
    width = HALF // points

    def body(rotation_ref, star_ref, own_ref, forward_ref, backward_ref, weight_ref, hold_ref, sem):
        load = pltpu.make_async_copy(own_ref, hold_ref.at[0], sem)
        load.start()
        shape = (orbitals, LANES)
        point = lane_block(shape, points)
        row = lax.broadcasted_iota(jnp.int32, shape, 0)
        columns = []
        for column in range(orbitals):
            total = jnp.zeros(shape, F32)
            for k in range(points):
                entry = rotation_ref[k].astype(F32)[:, column : column + 1]
                total = jnp.where(point == k, jnp.broadcast_to(entry, shape), total)
            columns.append(total)
        for shift in range(orbitals):
            forward = jnp.zeros(shape, F32)
            backward = jnp.zeros(shape, F32)
            for column in range(orbitals):
                here = lax.rem(row - shift + orbitals, orbitals) == column
                forward = jnp.where(here, columns[column], forward)
                moved = columns[column] if shift == 0 else pltpu.roll(columns[column], shift, 0)
                backward = jnp.where(row == column, moved, backward)
            forward_ref[shift] = forward
            backward_ref[shift] = backward
        star = jnp.zeros(shape, F32)
        for k in range(points):
            star = jnp.where(point == k, star_ref[k].astype(F32), star)
        same = [jnp.where(star == turn(star, width * step), 1.0, 0.0) for step in range(points)]
        count = functools.reduce(jnp.add, same)
        for step in range(points):
            weight_ref[step] = same[step] / count
        load.wait()

    return pl.pallas_call(
        body,
        out_shape=(
            jax.ShapeDtypeStruct((orbitals, orbitals, LANES), F32),
            jax.ShapeDtypeStruct((orbitals, orbitals, LANES), F32),
            jax.ShapeDtypeStruct((points, orbitals, LANES), F32),
            pltpu.VMEM((2,) + own_kernel.shape, own_kernel.dtype),
        ),
        in_specs=[VMEM, pl.BlockSpec(memory_space=pltpu.SMEM), ANY],
        out_specs=(VMEM,) * 4,
        scratch_shapes=[pltpu.SemaphoreType.DMA],
        compiler_params=PARAMS,
        cost_estimate=cost(0, 12 * orbitals * orbitals * LANES),
        name="tables",
    )(rotation, star_of, own_kernel)


def shards(kernel, dinv, source, rotation, star_of):
    tiles = lax.axis_size("tm")
    owners = lax.axis_size("mom")
    rows = source.shape[2]
    columns = source.shape[4]
    stages = tiles // 2
    chunks = columns // LANES
    items = chunks * SECTIONS
    trade = functools.partial(lax.ppermute, axis_name="tm", perm=[(i, i ^ 1) for i in range(tiles)])
    onward = functools.partial(lax.ppermute, axis_name="tm", perm=[(i, i + 2) for i in range(tiles - 2)])

    def deliver(messages):
        kept = [messages[0]]
        for step in range(1, owners):
            kept.append(lax.ppermute(messages[step], "mom", [(i, (i + step) % owners) for i in range(owners)]))
        return kept

    own_kernel = kernel.reshape(2 * rows, rows)
    other_kernel = trade(own_kernel)
    planes = source.reshape(2, rows, columns)
    stay = functools.partial(pltpu.with_memory_space_constraint, memory_space=pltpu.HBM)
    packed = pack_fronts(stay(planes), 0, owners, stay(dinv.reshape(2 * rows // LANES, LANES)))
    *tables, kernels = star_tables(rotation, star_of, stay(own_kernel))
    ready = pack_fronts(planes, 1, owners, after=(packed[0], tables[0]))
    kept = deliver(packed)
    got = trade(stack_other(kept, rows // owners, ready[:1]))
    front_a, front_b, factors, kernels = unpack_fronts(kept, got, rows, kernels, other_kernel)
    fronts = [(front_a, front_b)]
    kept = deliver(ready)

    incoming = [front_a] * DELAY
    before = (front_a, front_b)
    solved, chunked = [], []
    for time in range(items + DELAY * (stages - 1)):
        starting = {}
        for stage in range(stages):
            item = time - DELAY * stage
            if 0 <= item < items and item % SECTIONS == 0:
                starting[item // SECTIONS] = fronts[item // SECTIONS]
        before = tick(time, kernels, factors, starting, incoming[time], before, items, [])
        solved.append(before)
        incoming.append(onward(before[1]))
        chunk = time // SECTIONS + 1
        if 1 < chunk < chunks and time % SECTIONS == 0:
            kept = deliver(pack_fronts(planes, chunk, owners, after=before[1:]))
        if chunk < chunks and time % SECTIONS == SECTIONS - 1:
            fronts.append(unpack_fronts(kept, trade(stack_other(kept, rows // owners, (before[1], incoming[time + 1]))), rows))
        last = time - DELAY * (stages - 1)
        if last >= 0 and last % SECTIONS == SECTIONS - 1:
            candidates = []
            for stage in range(stages):
                candidates.extend(solved[last + DELAY * stage])
            chunked.append(deliver(star_stage(candidates, *tables, owners)))
    restored = []
    for back in chunked[:-1]:
        restored.append(restore(back, trade(stack_other(back, rows // owners, chunked[-1][1:9]))))
    back = chunked[-1]
    return assemble(restored, back, trade(stack_other(back, rows // owners, ())), columns).reshape(1, 2, rows, 1, columns)


def solution(mesh):
    in_specs = (
        P("tm", None, None, None),
        P("tm", None, None, "mom"),
        P("tm", None, None, "mom", None),
        P(),
        P(),
    )
    out_specs = P("tm", None, None, "mom", None)
    return jax.shard_map(shards, mesh=mesh, in_specs=in_specs, out_specs=out_specs, check_vma=False)
```

```python
import functools

import jax
import jax.numpy as jnp
from jax import lax
from jax.experimental import pallas as pl
from jax.experimental.pallas import tpu as pltpu
from jax.sharding import PartitionSpec as P

SECTIONS = 3
LANES = 128
HALF = LANES // 2
DELAY = 2
BLOCK = 256

VMEM = pl.BlockSpec(memory_space=pltpu.VMEM)
ANY = pl.BlockSpec(memory_space=pl.ANY)
F32 = jnp.float32
BF16 = jnp.bfloat16


PARAMS = pltpu.CompilerParams(vmem_limit_bytes=16 * 2**20)


def cost(flops, moved):
    return pl.CostEstimate(flops=flops, bytes_accessed=moved, transcendentals=0)


def lane_index(shape):
    return lax.broadcasted_iota(jnp.int32, shape, len(shape) - 1)


def turn(x, shift, half=HALF):
    shift %= half
    if shift == 0:
        return x
    inside = (lane_index(x.shape) & (half - 1)) >= shift
    return jnp.where(inside, pltpu.roll(x, shift, 1), pltpu.roll(x, shift + half, 1))


def lane_block(shape, owners):
    return (lane_index(shape) & (HALF - 1)) >> ((HALF // owners).bit_length() - 1)


def wrap(x, owners):
    return (x + 2 * owners) & (owners - 1)


def to_messages(blocks, owners, place, store):
    width = HALF // owners
    turned = [turn(block, width * q) for q, block in enumerate(blocks)]
    lanes = lane_block(blocks[0].shape, owners)
    for step in range(owners):
        panel = wrap(lanes - place - step, owners)
        message = turned[0]
        for q in range(1, owners):
            message = jnp.where(panel == q, turned[q], message)
        store(step, message.astype(BF16))


def from_messages(messages, owners, place):
    width = HALF // owners
    turned = [turn(message.astype(F32), width * ((owners - step) % owners)) for step, message in enumerate(messages)]
    lanes = lane_block(messages[0].shape, owners)
    panels = []
    for q in range(owners):
        step_of = wrap(place - lanes + q, owners)
        panel = turned[0]
        for step in range(1, owners):
            panel = jnp.where(step_of == step, turned[step], panel)
        panels.append(turn(panel, HALF - width * q))
    return panels


def pack_fronts(source, chunk, owners, dinv=None, after=()):
    rows, columns = source.shape[1:]
    panel = rows // owners
    leading = dinv is not None
    extra = 3 * dinv.shape[0] if leading else 0

    def body(source_ref, *refs):
        core = lax.rem(lax.axis_index("tm"), 2)
        place = lax.axis_index("mom")
        low = lane_index((panel, LANES)) < HALF
        out_refs = refs[1:] if leading else refs[len(after) :]
        if leading:
            dinv_hbm, plane_hbm = refs[0], source_ref
            source_ref, dinv_ref, sems = refs[1 + owners :]
            loads = [
                pltpu.make_async_copy(dinv_hbm, dinv_ref, sems.at[0]),
                pltpu.make_async_copy(plane_hbm, source_ref, sems.at[1]),
            ]
            for load in loads:
                load.start()
            loads[0].wait()
            loads[1].wait()
            first = dinv_ref[...].astype(BF16)
            rest = dinv_ref[...] - first.astype(F32)
            second = rest.astype(BF16)
            third = (rest - second.astype(F32)).astype(BF16)
            pieces = jnp.concatenate([first, second, third])
        for slot in range(2):
            half = core if slot == 0 else 1 - core
            start = pl.multiple_of(half * (columns // 2) + chunk // 2 * LANES, LANES)
            blocks = []
            for q in range(owners):
                real = source_ref[0, pl.ds(q * panel, panel), pl.ds(start, LANES)].astype(F32)
                imag = source_ref[1, pl.ds(q * panel, panel), pl.ds(start, LANES)].astype(F32)
                if chunk % 2 == 0:
                    blocks.append(jnp.where(low, real, pltpu.roll(imag, HALF, 1)))
                else:
                    blocks.append(jnp.where(low, pltpu.roll(real, HALF, 1), imag))

            def store(step, message):
                out_refs[step][pl.ds(slot * panel, panel), :] = message

            to_messages(blocks, owners, place, store)
        if leading:
            for step in range(owners):
                out_refs[step][pl.ds(2 * panel, extra), :] = pieces

    shapes = [jax.ShapeDtypeStruct((2 * panel + extra, LANES), BF16)] * owners
    scratch = []
    if leading:
        scratch = [pltpu.VMEM(source.shape, BF16), pltpu.VMEM(dinv.shape, F32), pltpu.SemaphoreType.DMA((2,))]
    given = (dinv,) if leading else tuple(after)
    return pl.pallas_call(
        body,
        out_shape=tuple(shapes),
        in_specs=[ANY] * 2 if leading else [VMEM] + [ANY] * len(after),
        out_specs=(VMEM,) * len(shapes),
        scratch_shapes=scratch,
        compiler_params=PARAMS,
        cost_estimate=cost(0, 2 * rows * columns * 2),
        name="pack",
    )(source, *given)


def stack_other(kept, panel, after):
    owners = len(kept)
    rest = kept[0].shape[0] - panel

    def body(*refs):
        for step in range(owners):
            refs[-1][step] = refs[step][pl.ds(panel, rest), :]

    return pl.pallas_call(
        body,
        out_shape=jax.ShapeDtypeStruct((owners, rest, LANES), BF16),
        in_specs=[VMEM] * owners + [ANY] * len(after),
        out_specs=VMEM,
        compiler_params=PARAMS,
        cost_estimate=cost(0, 4 * owners * rest * LANES),
        name="stack",
    )(*kept, *after)


def unpack_fronts(kept, got, rows, kernels=None, other_kernel=None):
    owners = len(kept)
    panel = rows // owners
    blocks = rows // LANES
    extra = kept[0].shape[0] - 2 * panel
    leading = kernels is not None

    def body(*refs):
        kept_refs, got_ref = refs[:owners], refs[owners]
        place = lax.axis_index("mom")
        if leading:
            other_ref, outs, hold_ref, sem = refs[owners + 2], refs[owners + 3 : owners + 6], refs[owners + 6], refs[owners + 7]
            load = pltpu.make_async_copy(other_ref, hold_ref.at[1], sem)
            load.start()
        else:
            outs = refs[owners + 1 :]
        for tile in range(2):
            first = slice(0, panel)
            messages = [kept_refs[step][first, :] if tile == 0 else got_ref[step, first, :] for step in range(owners)]
            panels = from_messages(messages, owners, place)
            for q in range(owners):
                outs[tile][pl.ds(q * panel, panel), :] = panels[q].astype(BF16)
            if not leading:
                continue
            last = slice(2 * panel, 2 * panel + extra) if tile == 0 else slice(panel, panel + extra)
            pieces = jnp.concatenate([kept_refs[step][last, :] if tile == 0 else got_ref[step, last, :] for step in range(owners)])
            shape = (owners * extra, LANES)
            row = lax.broadcasted_iota(jnp.int32, shape, 0)
            owner = wrap(place - row // extra, owners)
            wanted = owner == lane_block(shape, owners)
            inner = lax.rem(lax.rem(row, extra), 2 * blocks)
            sign = jnp.where(lane_index(shape) < HALF, -1.0, 1.0)
            for part in range(2):
                scale = jnp.ones(shape, F32) if part == 0 else sign
                for block in range(blocks):
                    pick = jnp.where(wanted & (inner == part * blocks + block), scale, 0.0).astype(BF16)
                    spread = lax.dot_general(pieces, pick, (((0,), (0,)), ((), ())), preferred_element_type=F32)
                    outs[2][tile, part, pl.ds(block * LANES, LANES), :] = spread
        if leading:
            load.wait()

    shapes = [jax.ShapeDtypeStruct((rows, LANES), BF16)] * 2
    given = [*kept, got]
    aliases = {}
    if leading:
        shapes += [pltpu.VMEM((2, 2, rows, LANES), F32), pltpu.VMEM(kernels.shape, kernels.dtype)]
        aliases = {len(given): 3}
        given += [kernels, other_kernel]
    return pl.pallas_call(
        body,
        out_shape=tuple(shapes),
        in_specs=[VMEM] * (owners + 1) + ([VMEM, ANY] if leading else []),
        out_specs=(VMEM,) * len(shapes),
        scratch_shapes=[pltpu.SemaphoreType.DMA] if leading else [],
        input_output_aliases=aliases,
        compiler_params=PARAMS,
        cost_estimate=cost(0, 8 * rows * LANES),
        name="unpack_first" if leading else "unpack_next",
    )(*given)


def tick(time, kernels, factors, fronts, incoming, before, items, after):
    rows = incoming.shape[0]
    block = min(rows, BLOCK)
    chunks = sorted(fronts)

    def body(kernel_ref, factor_ref, in_ref, *refs):
        front_refs = refs[: 2 * len(chunks)]
        before_a, before_b, out_a, out_b, base_a, base_b = refs[2 * len(chunks) :][:2] + refs[-4:]
        index = lax.axis_index("tm")
        core = lax.rem(index, 2)
        chip = index // 2
        item = time - DELAY * chip
        section = lax.rem(item + SECTIONS * 64, SECTIONS)
        sign = jnp.where(lane_index((block, LANES)) < HALF, -1.0, 1.0).astype(F32)

        def finish(slot, start, total, target):
            span = pl.ds(start, block)
            turned = pltpu.roll(total, HALF, 1)
            target[span, :] = (factor_ref[slot, 0, span, :] * total + factor_ref[slot, 1, span, :] * turned).astype(BF16)

        def product(slot, start, x_ref):
            real = jnp.dot(kernel_ref[slot, pl.ds(start, block), :], x_ref[...], preferred_element_type=F32)
            imag = jnp.dot(kernel_ref[slot, pl.ds(rows + start, block), :], x_ref[...], preferred_element_type=F32)
            return real + pltpu.roll(imag, HALF, 1) * sign

        @pl.when((item >= 0) & (item < items))
        def _():
            for place, chunk in enumerate(chunks):
                for parity in range(2):

                    @pl.when((item == chunk * SECTIONS) & (core == parity))
                    def _():
                        base_a[...] = front_refs[2 * place + parity][...]
                        base_b[...] = front_refs[2 * place + 1 - parity][...]

            @pl.when(section > 0)
            def _():
                base_a[...] = before_a[...]
                base_b[...] = before_b[...]

            @pl.when(chip == 0)
            def _():
                for start in range(0, rows, block):
                    finish(core, start, base_a[pl.ds(start, block), :].astype(F32), out_a)

            @pl.when(chip > 0)
            def _():
                for start in range(0, rows, block):
                    total = base_a[pl.ds(start, block), :].astype(F32) + product(core, start, in_ref)
                    finish(core, start, total, out_a)

            for start in range(0, rows, block):
                total = base_b[pl.ds(start, block), :].astype(F32) + product(1 - core, start, out_a)
                finish(1 - core, start, total, out_b)

    shape = jax.ShapeDtypeStruct((rows, LANES), BF16)
    given = [front for chunk in chunks for front in fronts[chunk]]
    return pl.pallas_call(
        body,
        out_shape=(shape, shape),
        in_specs=[VMEM] * (5 + len(given)) + [ANY] * len(after),
        out_specs=(VMEM, VMEM),
        scratch_shapes=[pltpu.VMEM((rows, LANES), BF16)] * 2,
        compiler_params=PARAMS,
        cost_estimate=cost(2 * rows * rows * 64, rows * LANES),
        name="tick",
    )(kernels, factors, incoming, *given, *before, *after)


def star_stage(candidates, forward, backward, weights, owners):
    rows = candidates[0].shape[0]
    stages = len(candidates) // 2
    panel = rows // owners
    orbitals = backward.shape[0]
    width = HALF // owners

    def body(*refs):
        inputs = refs[: len(candidates)]
        forward_ref, backward_ref, weight_ref = refs[len(candidates) : len(candidates) + 3]
        out_refs = refs[len(candidates) + 3 : len(candidates) + 3 + owners]
        green_ref = refs[-1]
        index = lax.axis_index("tm")
        core = lax.rem(index, 2)
        chip = index // 2
        place = lax.axis_index("mom")
        for stage in range(stages):
            for parity in range(2):

                @pl.when((chip == stage) & (core == parity))
                def _():
                    for slot in range(2):
                        green_ref[slot] = inputs[2 * stage + (parity + slot) % 2][...]

        def mix(x, table_ref):
            groups = x.reshape(panel // orbitals, orbitals, LANES)
            total = groups * table_ref[0]
            for shift in range(1, orbitals):
                total += pltpu.roll(groups, shift, 1) * table_ref[shift]
            return total.reshape(panel, LANES)

        for slot in range(2):
            blocks = []
            for q in range(owners):
                rotated = mix(green_ref[slot, pl.ds(q * panel, panel), :].astype(F32), forward_ref)
                green = rotated * weight_ref[0, :1]
                for step in range(1, owners):
                    green += turn(rotated, width * step) * weight_ref[step, :1]
                square = green * green
                sigma = (square + pltpu.roll(square, HALF, 1)) * green
                blocks.append(mix(sigma, backward_ref))

            def store(step, message):
                out_refs[step][pl.ds(slot * panel, panel), :] = message

            to_messages(blocks, owners, place, store)

    shape = jax.ShapeDtypeStruct((2 * panel, LANES), BF16)
    return pl.pallas_call(
        body,
        out_shape=(shape,) * owners,
        in_specs=[VMEM] * (len(candidates) + 3),
        out_specs=(VMEM,) * owners,
        scratch_shapes=[pltpu.VMEM((2, rows, LANES), BF16)],
        compiler_params=PARAMS,
        cost_estimate=cost(0, 16 * rows * LANES),
        name="stars",
    )(*candidates, forward, backward, weights)


def restore(kept, got):
    owners = len(kept)
    panel = kept[0].shape[0] // 2

    def body(*refs):
        place = lax.axis_index("mom")
        for side in range(2):
            messages = [refs[d][pl.ds(0, panel), :] if side == 0 else refs[owners][d] for d in range(owners)]
            for q, block in enumerate(from_messages(messages, owners, place)):
                refs[-1][side, pl.ds(q * panel, panel), :] = block.astype(BF16)

    return pl.pallas_call(
        body,
        out_shape=jax.ShapeDtypeStruct((2, owners * panel, LANES), BF16),
        in_specs=[VMEM] * (owners + 1),
        out_specs=VMEM,
        compiler_params=PARAMS,
        cost_estimate=cost(0, 8 * owners * panel * LANES),
        name="restore",
    )(*kept, got)


def assemble(restored, kept, got, columns):
    owners = len(kept)
    panel = kept[0].shape[0] // 2
    count = len(restored)

    def body(*refs):
        out_ref = refs[-1]
        core = lax.rem(lax.axis_index("tm"), 2)
        place = lax.axis_index("mom")
        low = lane_index((panel, LANES)) < HALF
        for side in range(2):
            half = core if side == 0 else 1 - core
            messages = [refs[count + d][pl.ds(0, panel), :] if side == 0 else refs[count + owners][d] for d in range(owners)]
            last = from_messages(messages, owners, place)
            for pair in range((count + 1) // 2):
                start = pl.multiple_of(half * (columns // 2) + pair * LANES, LANES)
                for q in range(owners):
                    span = pl.ds(q * panel, panel)
                    first = refs[2 * pair][side, span, :].astype(F32)
                    second = last[q] if 2 * pair + 1 == count else refs[2 * pair + 1][side, span, :].astype(F32)
                    out_ref[0, span, pl.ds(start, LANES)] = jnp.where(low, first, pltpu.roll(second, HALF, 1)).astype(BF16)
                    out_ref[1, span, pl.ds(start, LANES)] = jnp.where(low, pltpu.roll(first, HALF, 1), second).astype(BF16)

    given = [*restored, *kept, got]
    return pl.pallas_call(
        body,
        out_shape=jax.ShapeDtypeStruct((2, owners * panel, columns), BF16),
        in_specs=[VMEM] * len(given),
        out_specs=VMEM,
        compiler_params=PARAMS,
        cost_estimate=cost(0, 8 * owners * panel * columns),
        name="assemble",
    )(*given)


def star_tables(rotation, star_of, own_kernel):
    points, orbitals = rotation.shape[:2]
    width = HALF // points

    def body(rotation_ref, star_ref, own_ref, forward_ref, backward_ref, weight_ref, hold_ref, sem):
        load = pltpu.make_async_copy(own_ref, hold_ref.at[0], sem)
        load.start()
        shape = (orbitals, LANES)
        point = lane_block(shape, points)
        row = lax.broadcasted_iota(jnp.int32, shape, 0)
        columns = []
        for column in range(orbitals):
            total = jnp.zeros(shape, F32)
            for k in range(points):
                entry = rotation_ref[k][:, column : column + 1]
                total = jnp.where(point == k, jnp.broadcast_to(entry, shape), total)
            columns.append(total)
        for shift in range(orbitals):
            forward = jnp.zeros(shape, F32)
            backward = jnp.zeros(shape, F32)
            for column in range(orbitals):
                here = lax.rem(row - shift + orbitals, orbitals) == column
                forward = jnp.where(here, columns[column], forward)
                moved = columns[column] if shift == 0 else pltpu.roll(columns[column], shift, 0)
                backward = jnp.where(row == column, moved, backward)
            forward_ref[shift] = forward
            backward_ref[shift] = backward
        star = jnp.zeros(shape, F32)
        for k in range(points):
            star = jnp.where(point == k, star_ref[k].astype(F32), star)
        same = [jnp.where(star == turn(star, width * step), 1.0, 0.0) for step in range(points)]
        count = functools.reduce(jnp.add, same)
        for step in range(points):
            weight_ref[step] = same[step] / count
        load.wait()

    return pl.pallas_call(
        body,
        out_shape=(
            jax.ShapeDtypeStruct((orbitals, orbitals, LANES), F32),
            jax.ShapeDtypeStruct((orbitals, orbitals, LANES), F32),
            jax.ShapeDtypeStruct((points, orbitals, LANES), F32),
            pltpu.VMEM((2,) + own_kernel.shape, own_kernel.dtype),
        ),
        in_specs=[VMEM, pl.BlockSpec(memory_space=pltpu.SMEM), ANY],
        out_specs=(VMEM,) * 4,
        scratch_shapes=[pltpu.SemaphoreType.DMA],
        compiler_params=PARAMS,
        cost_estimate=cost(0, 12 * orbitals * orbitals * LANES),
        name="tables",
    )(rotation.astype(F32), star_of, own_kernel)


def shards(kernel, dinv, source, rotation, star_of):
    tiles = lax.axis_size("tm")
    owners = lax.axis_size("mom")
    rows = source.shape[2]
    columns = source.shape[4]
    stages = tiles // 2
    chunks = columns // LANES
    items = chunks * SECTIONS
    trade = functools.partial(lax.ppermute, axis_name="tm", perm=[(i, i ^ 1) for i in range(tiles)])
    onward = functools.partial(lax.ppermute, axis_name="tm", perm=[(i, i + 2) for i in range(tiles - 2)])

    def deliver(messages):
        kept = [messages[0]]
        for step in range(1, owners):
            kept.append(lax.ppermute(messages[step], "mom", [(i, (i + step) % owners) for i in range(owners)]))
        return kept

    own_kernel = kernel.reshape(2 * rows, rows)
    other_kernel = trade(own_kernel)
    planes = source.reshape(2, rows, columns)
    stay = functools.partial(pltpu.with_memory_space_constraint, memory_space=pltpu.HBM)
    packed = pack_fronts(stay(planes), 0, owners, stay(dinv.reshape(2 * rows // LANES, LANES)))
    *tables, kernels = star_tables(rotation, star_of, stay(own_kernel))
    ready = pack_fronts(planes, 1, owners, after=(packed[0], tables[0]))
    kept = deliver(packed)
    got = trade(stack_other(kept, rows // owners, ready[:1]))
    front_a, front_b, factors, kernels = unpack_fronts(kept, got, rows, kernels, other_kernel)
    fronts = [(front_a, front_b)]
    kept = deliver(ready)

    incoming = [front_a] * DELAY
    before = (front_a, front_b)
    solved, chunked = [], []
    for time in range(items + DELAY * (stages - 1)):
        starting = {}
        for stage in range(stages):
            item = time - DELAY * stage
            if 0 <= item < items and item % SECTIONS == 0:
                starting[item // SECTIONS] = fronts[item // SECTIONS]
        before = tick(time, kernels, factors, starting, incoming[time], before, items, [])
        solved.append(before)
        incoming.append(onward(before[1]))
        chunk = time // SECTIONS + 1
        if 1 < chunk < chunks and time % SECTIONS == 0:
            kept = deliver(pack_fronts(planes, chunk, owners, after=before[1:]))
        if chunk < chunks and time % SECTIONS == SECTIONS - 1:
            fronts.append(unpack_fronts(kept, trade(stack_other(kept, rows // owners, (before[1], incoming[time + 1]))), rows))
        last = time - DELAY * (stages - 1)
        if last >= 0 and last % SECTIONS == SECTIONS - 1:
            candidates = []
            for stage in range(stages):
                candidates.extend(solved[last + DELAY * stage])
            chunked.append(deliver(star_stage(candidates, *tables, owners)))
    restored = []
    for back in chunked[:-1]:
        restored.append(restore(back, trade(stack_other(back, rows // owners, chunked[-1][1:9]))))
    back = chunked[-1]
    return assemble(restored, back, trade(stack_other(back, rows // owners, ())), columns).reshape(1, 2, rows, 1, columns)


def solution(mesh):
    in_specs = (
        P("tm", None, None, None),
        P("tm", None, None, "mom"),
        P("tm", None, None, "mom", None),
        P(),
        P(),
    )
    out_specs = P("tm", None, None, "mom", None)
    return jax.shard_map(shards, mesh=mesh, in_specs=in_specs, out_specs=out_specs, check_vma=False)
```
